512 devices in a mesh: row: 32 (over z, core), col: 16 (over y, x).
Axes of the slice: x: 4, y: 4, z: 16, core: 2. Of those that a mesh axis runs over, the one named last changes fastest.
Arguments:
- queries: bfloat16 [32, 1024, 256], P('row', 'col'), may hold values from -32 to 32
- key_lanes: bfloat16 [16, 2048, 256], P('col'), may hold values from -6 to 6
- values: bfloat16 [16, 2048, 256], P('col'), may hold values from -6 to 6
- grad_out: bfloat16 [32, 1024, 256], P('row', 'col'), may hold values from -6 to 6
- pattern: int32 [32, 16, 28], P('row', 'col'), may hold values from 0 to 127, as said below
- counts: int32 [32, 16], P('row', 'col'), may hold values from 8 to 28
Outputs:
- attended: bfloat16 [32, 1024, 256], P('row', 'col')
- grad_queries: bfloat16 [32, 1024, 256], P('row', 'col')
- grad_keys: bfloat16 [16, 2048, 256], P('col', 'row')
- grad_values: bfloat16 [16, 2048, 256], P('col', 'row')
The draws below stay inside these ranges and needn't reach their ends.
Inputs may be any that keep to these rules, and one draw needn't show every extreme that they name: The entries of pattern[g, c] are distinct; only the first counts[g, c] of them are used, and among those every query block of the group appears.
All inputs are finite; a program needn't handle non-finite values.
Results may differ from the reference program's by a relative error of at most 0.025.
Values may be sent and summed in bfloat16 or wider, within the bound.
A program may use at most 64 MiB of HBM per device.

```python
import math
import jax
import jax.numpy as jnp
from jax import lax

D = 256
H = 8
HD = 32
BLK = 128
QB = 8
QG = 1024
KBS = 16
KS = 2048
MAXP = 28
N_ROW = 32
N_COL = 16


def pattern_tables(key):
    key = jax.random.fold_in(key, 101)
    order_key, count_key, choose_key, noise_key = jax.random.split(key, 4)
    order = jax.random.permutation(order_key, N_ROW)
    urban = order < max(1, N_ROW // 8)
    rural = jax.random.randint(count_key, (N_ROW, N_COL), max(QB, MAXP // 7), MAXP // 3 + 1)
    counts = jnp.where(urban[:, None], MAXP, rural).astype(jnp.int32)
    chosen = jax.random.randint(choose_key, (N_ROW, N_COL, QB), 0, KBS)
    cell_ids = jnp.arange(QB * KBS, dtype=jnp.int32)
    picked = jnp.take(chosen, cell_ids // KBS, axis=2) == (cell_ids % KBS)[None, None, :]
    noise = jax.random.randint(noise_key, (N_ROW, N_COL, QB * KBS), 0, 2 ** 16)
    ranks = noise * (QB * KBS) + cell_ids[None, None, :] - picked.astype(jnp.int32) * 2 ** 28
    cells = jnp.argsort(ranks, axis=-1, stable=True)[:, :, :MAXP].astype(jnp.int32)
    return (cells, counts)


def lanes_drawn(key):
    key = jax.random.fold_in(key, 202)
    return jnp.clip(jax.random.normal(key, (N_COL, KS, D), jnp.float32), -6.0, 6.0)


def draw_pattern(key, part):
    cells, counts = pattern_tables(key)
    return cells


def draw_counts(key, part):
    cells, counts = pattern_tables(key)
    return counts


def draw_key_lanes(key, part):
    return lanes_drawn(key).astype(jnp.bfloat16)


def draw_queries(key, part):
    key = jax.random.fold_in(key, 303)
    base = jnp.clip(jax.random.normal(key, (N_ROW, QG, D), jnp.float32), -6.0, 6.0)
    return base.astype(jnp.bfloat16)


def levels(rng, extent, cuts, smallest, high):
    loudness, own = 1.0, jax.random.fold_in(rng, 6)
    for position, parts in cuts:
        draws = jnp.exp(jax.random.uniform(jax.random.fold_in(own, position), (parts,), jnp.float32, smallest / len(cuts), high / len(cuts)))
        loudness = loudness * jnp.repeat(draws, extent[position] // parts).reshape([-1 if axis == position else 1 for axis in range(len(extent))])
    return loudness


def scatter_about(key, shape, width, limit, cuts=(), kind=jnp.bfloat16):
    level = levels(key, shape, cuts, -0.22, 0.18) if cuts else 1.0
    drawn = jax.random.normal(key, shape, jnp.float32) * width * level
    return jnp.minimum(jnp.maximum(drawn, -limit), limit).astype(kind)


def setup_inputs(seed: int = 0) -> dict:
    key_of = jax.random.split(jax.random.key(seed), 7)
    return {
        "queries": draw_queries(jax.random.fold_in(key_of[6], 71), 0),
        "key_lanes": draw_key_lanes(jax.random.fold_in(key_of[6], 71), 0),
        "values": scatter_about(key_of[2], (N_COL, KS, D), 1.0, 6.0, ((0, 16),)),
        "grad_out": scatter_about(key_of[3], (N_ROW, QG, D), 1.0, 6.0, ((0, 32), (1, 16))),
        "pattern": draw_pattern(jax.random.fold_in(key_of[6], 71), 0),
        "counts": draw_counts(jax.random.fold_in(key_of[6], 71), 0),
    }


neg_fill = -1e+30

def head_split(matrix):
    return matrix.reshape(matrix.shape[0], H, HD)

def rounded(part):
    return lax.optimization_barrier(part.astype(jnp.bfloat16)).astype(jnp.float32)

def block_scores(q_block, k_block):
    q_heads = head_split(q_block.astype(jnp.float32))
    k_heads = head_split(k_block.astype(jnp.float32))
    return jnp.einsum('qhd,khd->hqk', q_heads, k_heads) / math.sqrt(HD)

def local_max(group_q, lanes_c, cell_list, pair_count):

    def add_pair(i, best_rows):
        cell = cell_list[i]
        q_start = (cell // KBS * BLK).astype(jnp.int32)
        k_start = (cell % KBS * BLK).astype(jnp.int32)
        scores = block_scores(lax.dynamic_slice_in_dim(group_q, q_start, BLK, 0), lax.dynamic_slice_in_dim(lanes_c, k_start, BLK, 0))
        previous = lax.dynamic_slice_in_dim(best_rows, q_start, BLK, 0)
        return lax.dynamic_update_slice_in_dim(best_rows, jnp.maximum(previous, lax.optimization_barrier(jnp.max(scores, axis=2)).T), q_start, 0)
    start_max = jnp.full((QG, H), neg_fill, jnp.float32)
    return lax.fori_loop(jnp.int32(0), pair_count, add_pair, start_max)

def forward_sums(group_q, lanes_c, values_c, cell_list, pair_count, row_max):

    def add_pair(i, carry):
        totals, weighted = carry
        cell = cell_list[i]
        q_start = (cell // KBS * BLK).astype(jnp.int32)
        k_start = (cell % KBS * BLK).astype(jnp.int32)
        scores = block_scores(lax.dynamic_slice_in_dim(group_q, q_start, BLK, 0), lax.dynamic_slice_in_dim(lanes_c, k_start, BLK, 0))
        top = lax.dynamic_slice_in_dim(row_max, q_start, BLK, 0)
        probs = jnp.exp(scores - top.T[:, :, None])
        probs_bf = probs.astype(jnp.bfloat16)
        v_block = head_split(lax.dynamic_slice_in_dim(values_c, k_start, BLK, 0).astype(jnp.float32))
        mixed = jnp.einsum('hqk,khd->qhd', probs_bf.astype(jnp.float32), v_block).reshape(BLK, D)
        old_tot = lax.dynamic_slice_in_dim(totals, q_start, BLK, 0)
        old_wei = lax.dynamic_slice_in_dim(weighted, q_start, BLK, 0)
        totals = lax.dynamic_update_slice_in_dim(totals, old_tot + lax.optimization_barrier(jnp.sum(probs, axis=2)).T, q_start, 0)
        weighted = lax.dynamic_update_slice_in_dim(weighted, old_wei + mixed, q_start, 0)
        return (totals, weighted)
    start = (jnp.zeros((QG, H), jnp.float32), jnp.zeros((QG, D), jnp.float32))
    return lax.fori_loop(jnp.int32(0), pair_count, add_pair, start)

def backward(group_q, group_g, lanes_c, values_c, cell_list, pair_count, log_total, row_dots):
    scale = 1.0 / math.sqrt(HD)

    def add_pair(i, carry):
        grad_q, grad_k, grad_v = carry
        cell = cell_list[i]
        q_start = (cell // KBS * BLK).astype(jnp.int32)
        k_start = (cell % KBS * BLK).astype(jnp.int32)
        q_block = lax.dynamic_slice_in_dim(group_q, q_start, BLK, 0)
        k_block = lax.dynamic_slice_in_dim(lanes_c, k_start, BLK, 0)
        v_block = lax.dynamic_slice_in_dim(values_c, k_start, BLK, 0)
        g_block = lax.dynamic_slice_in_dim(group_g, q_start, BLK, 0)
        scores = block_scores(q_block, k_block)
        norm_rows = lax.dynamic_slice_in_dim(log_total, q_start, BLK, 0)
        dot_rows = lax.dynamic_slice_in_dim(row_dots, q_start, BLK, 0)
        weights = jnp.exp(scores - norm_rows.T[:, :, None])
        weights_bf = weights.astype(jnp.bfloat16).astype(jnp.float32)
        g_heads = head_split(g_block.astype(jnp.float32))
        v_heads = head_split(v_block.astype(jnp.float32))
        q_heads = head_split(q_block.astype(jnp.float32))
        k_heads = head_split(k_block.astype(jnp.float32))
        new_v = jnp.einsum('hqk,qhd->khd', weights_bf, g_heads).reshape(BLK, D)
        dprob = jnp.einsum('qhd,khd->hqk', g_heads, v_heads)
        dscore = weights * (dprob - dot_rows.T[:, :, None])
        dscore_bf = dscore.astype(jnp.bfloat16).astype(jnp.float32)
        new_q = jnp.einsum('hqk,khd->qhd', dscore_bf, k_heads).reshape(BLK, D) * scale
        new_k = jnp.einsum('hqk,qhd->khd', dscore_bf, q_heads).reshape(BLK, D) * scale
        grad_q = lax.dynamic_update_slice_in_dim(grad_q, lax.dynamic_slice_in_dim(grad_q, q_start, BLK, 0) + new_q, q_start, 0)
        grad_k = lax.dynamic_update_slice_in_dim(grad_k, lax.dynamic_slice_in_dim(grad_k, k_start, BLK, 0) + new_k, k_start, 0)
        grad_v = lax.dynamic_update_slice_in_dim(grad_v, lax.dynamic_slice_in_dim(grad_v, k_start, BLK, 0) + new_v, k_start, 0)
        return (grad_q, grad_k, grad_v)
    start = (jnp.zeros((QG, D), jnp.float32), jnp.zeros((KS, D), jnp.float32), jnp.zeros((KS, D), jnp.float32))
    return lax.fori_loop(jnp.int32(0), pair_count, add_pair, start)

def reference(queries, key_lanes, values, grad_out, pattern, counts):

    def per_group(carry, inputs):
        sum_k, sum_v = carry
        group_q, group_g, cells_g, counts_g = inputs

        def shard_max(best_rows, shard):
            lanes_c, cell_list, pair_count = shard
            return (jnp.maximum(best_rows, local_max(group_q, lanes_c, cell_list, pair_count)), None)
        row_max = lax.scan(shard_max, jnp.full((QG, H), neg_fill, jnp.float32), (key_lanes, cells_g, counts_g))[0]

        def shard_sums(acc_pair, shard):
            lanes_c, values_c, cell_list, pair_count = shard
            totals, weighted = forward_sums(group_q, lanes_c, values_c, cell_list, pair_count, row_max)
            return ((acc_pair[0] + totals, acc_pair[1] + weighted), None)
        start = (jnp.zeros((QG, H), jnp.float32), jnp.zeros((QG, D), jnp.float32))
        totals, weighted = lax.scan(shard_sums, start, (key_lanes, values, cells_g, counts_g))[0]
        log_total = row_max + jnp.log(totals)
        normed = (head_split(weighted) / totals[:, :, None]).reshape(QG, D)
        row_dots = lax.optimization_barrier(jnp.sum(head_split(group_g.astype(jnp.float32)) * head_split(normed), axis=2))

        def shard_back(grad_q, shard):
            lanes_c, values_c, cell_list, pair_count = shard
            part_q, part_k, part_v = backward(group_q, group_g, lanes_c, values_c, cell_list, pair_count, log_total, row_dots)
            return (grad_q + part_q, (part_k, part_v))
        grad_q, (parts_k, parts_v) = lax.scan(shard_back, jnp.zeros((QG, D), jnp.float32), (key_lanes, values, cells_g, counts_g))
        return ((sum_k + rounded(parts_k), sum_v + rounded(parts_v)), (normed.astype(jnp.bfloat16), grad_q.astype(jnp.bfloat16)))
    start = (jnp.zeros((N_COL, KS, D), jnp.float32), jnp.zeros((N_COL, KS, D), jnp.float32))
    (sum_k, sum_v), (attended, grad_queries) = lax.scan(per_group, start, (queries, grad_out, pattern, counts))
    return (attended, grad_queries, sum_k.astype(jnp.bfloat16), sum_v.astype(jnp.bfloat16))
```

```python
import functools
import math

import jax
import jax.numpy as jnp
from jax import lax
from jax.experimental import pallas as pl
from jax.experimental.pallas import tpu as pltpu
from jax.sharding import PartitionSpec as P

D = 256
H = 8
HD = 32
BLK = 128
HALF = D // 2
HH = H // 2
MESH = pl.DeviceIdType.MESH
SCALE = 1.0 / math.sqrt(HD)
LOG2E = math.log2(math.e)
SCALE2 = SCALE * LOG2E
NEG = -1e30
VMEM_LIMIT = 56 * 1024 * 1024

vmem = pl.BlockSpec(memory_space=pltpu.VMEM)
smem = pl.BlockSpec(memory_space=pltpu.SMEM)


def call(kernel, name, out_shape, n_smem, n_vmem, scratch, collective_id=None):
    return pl.pallas_call(
        kernel,
        name=name,
        out_shape=out_shape,
        in_specs=[smem] * n_smem + [vmem] * n_vmem,
        out_specs=jax.tree.map(lambda _: vmem, out_shape),
        scratch_shapes=scratch,
        compiler_params=pltpu.CompilerParams(
            collective_id=collective_id,
            has_side_effects=collective_id is not None,
            vmem_limit_bytes=VMEM_LIMIT,
        ),
    )


def meet(peers):
    barrier = pltpu.get_barrier_semaphore()
    for peer in peers:
        pl.semaphore_signal(barrier, inc=1, device_id=peer, device_id_type=MESH)
    pl.semaphore_wait(barrier, len(peers))


def remote(src, dst, send_sem, recv_sem, device):
    return pltpu.make_async_remote_copy(
        src_ref=src,
        dst_ref=dst,
        send_sem=send_sem,
        recv_sem=recv_sem,
        device_id=device,
        device_id_type=MESH,
    )


def others(me, n):
    return [lax.rem(me + k, n) for k in range(1, n)]


def senders(me, n):
    return [lax.rem(me + n - k, n) for k in range(1, n)]


def head_mask(h):
    lane = lax.broadcasted_iota(jnp.int32, (BLK, D), 1)
    return jnp.where((lane >= h * HD) & (lane < (h + 1) * HD), 1.0, 0.0).astype(jnp.bfloat16)


def block_diagonal(refs, outs):
    blocks = outs[0].shape[0]
    for h in range(H):
        mask = head_mask(h)

        def one(b, carry):
            rows = pl.ds(pl.multiple_of(b * BLK, BLK), BLK)
            for ref, out in zip(refs, outs):
                out[b, h * BLK : (h + 1) * BLK, :] = ref[rows, :] * mask
            return carry

        lax.fori_loop(0, blocks, one, 0)


def dot_nt(a, b):
    return lax.dot_general(a, b, (((1,), (1,)), ((), ())), preferred_element_type=jnp.float32)


def dot(a, b):
    return jnp.dot(a, b, preferred_element_type=jnp.float32)


def gather_kernel(n, q_ref, g_ref, k_ref, v_ref, qo, go, kt, vt, send_sem, recv_sem):
    row, me = lax.axis_index("row"), lax.axis_index("col")
    peers = others(me, n)
    meet([(row, p) for p in peers])
    sends = []
    for i, (src, dst) in enumerate(((q_ref, qo), (g_ref, go))):
        for p in peers:
            copy = remote(src, dst.at[me], send_sem.at[i, p], recv_sem.at[i, me], (row, p))
            copy.start()
            sends.append(copy)
    qo[me] = q_ref[...]
    go[me] = g_ref[...]

    def turn(b, carry):
        rows = pl.ds(pl.multiple_of(b * BLK, BLK), BLK)
        kt[:, rows] = k_ref[rows, :].T
        vt[:, rows] = v_ref[rows, :].T
        return carry

    lax.fori_loop(0, k_ref.shape[0] // BLK, turn, 0)
    for i, (src, dst) in enumerate(((q_ref, qo), (g_ref, go))):
        for p in senders(me, n):
            remote(src, dst.at[p], send_sem.at[i, p], recv_sem.at[i, p], (row, p)).wait_recv()
    for copy in sends:
        copy.wait_send()


def forward_kernel(key_blocks, cells, count, q_ref, k_ref, vt_ref, part, stat, qbd, acc, top, tot):
    block_diagonal((q_ref,), (qbd,))
    acc[...] = jnp.zeros_like(acc)
    tot[...] = jnp.zeros_like(tot)
    top[...] = jnp.full_like(top, NEG)

    def pair(j, carry):
        cell = cells[0, j]
        qb = cell // key_blocks
        q_at = pl.ds(pl.multiple_of(qb * BLK, BLK), BLK)
        k_at = pl.ds(pl.multiple_of(cell % key_blocks * BLK, BLK), BLK)
        scores = dot_nt(k_ref[k_at, :], qbd[qb])
        old = top[:, q_at]
        best = [
            jnp.max(scores[:, h * BLK : (h + 1) * BLK], axis=0, keepdims=True) for h in range(H)
        ]
        new = jnp.maximum(old, jnp.concatenate(best, axis=0) * SCALE2)
        fade = jnp.exp2(old - new)
        top[:, q_at] = new
        sums = []
        for h in range(H):
            probs = jnp.exp2(scores[:, h * BLK : (h + 1) * BLK] * SCALE2 - new[h : h + 1])
            sums.append(jnp.sum(probs, axis=0, keepdims=True))
            at = slice(h * HD, (h + 1) * HD)
            mixed = dot(vt_ref[at, k_at], probs.astype(jnp.bfloat16))
            acc[at, q_at] = acc[at, q_at] * fade[h : h + 1] + mixed
        tot[:, q_at] = tot[:, q_at] * fade + jnp.concatenate(sums, axis=0)
        return carry

    lax.fori_loop(0, count[0, 0], pair, 0)
    for b in range(qbd.shape[0]):
        lanes = slice(b * BLK, (b + 1) * BLK)
        for half in range(2):
            part[2 * b + half] = acc[half * HALF : (half + 1) * HALF, lanes].astype(jnp.bfloat16)
            heads = slice(half * HH, (half + 1) * HH)
            stat[2 * b + half] = jnp.concatenate([top[heads, lanes], tot[heads, lanes]], axis=0)


def swap_halves(own, out, got, mine, send_sem, recv_sem, row, me):
    half = lax.rem(me, 2)
    rows = BLK // 2
    own_at = pl.ds(pl.multiple_of(half * rows, rows), rows)
    other_at = pl.ds(pl.multiple_of((1 - half) * rows, rows), rows)
    mine[...] = own
    copy = remote(mine.at[other_at], got, send_sem, recv_sem, (row, me + 1 - 2 * half))
    copy.start()

    def finish():
        out[:, pl.ds(pl.multiple_of(half * HALF, HALF), HALF)] = mine[own_at, :]
        copy.wait_recv()
        out[:, pl.ds(pl.multiple_of((1 - half) * HALF, HALF), HALF)] = got[...]
        copy.wait_send()

    return finish


def combine_kernel(
    n, part, stat, g_ref, att, logs, parts, stats, mine, got, part_sems, stat_sems, log_sems, swap_sems
):
    row, me = lax.axis_index("row"), lax.axis_index("col")
    peers, sources = others(me, n), senders(me, n)
    meet([(row, p) for p in peers])
    sends = []
    for src, dst, sems in ((stat, stats, stat_sems), (part, parts, part_sems)):
        for p in peers:
            copy = remote(src.at[p], dst.at[me], sems.at[0, p], sems.at[1, me], (row, p))
            copy.start()
            sends.append(copy)
    block, half = me // 2, lax.rem(me, 2)
    grad = g_ref[
        pl.ds(pl.multiple_of(block * BLK, BLK), BLK), pl.ds(pl.multiple_of(half * HALF, HALF), HALF)
    ]
    grad = grad.astype(jnp.float32).T.reshape(HH, HD, BLK)
    stats[me] = stat[me]
    for p in sources:
        remote(stat.at[p], stats.at[p], stat_sems.at[0, p], stat_sems.at[1, p], (row, p)).wait_recv()
    every = stats[...]
    top = jnp.max(every[:, :HH], axis=0)
    tot = jnp.sum(every[:, HH:] * jnp.exp2(every[:, :HH] - top[None]), axis=0)

    def share(source, ref):
        fade = jnp.exp2(stats[source][:HH] - top)
        return ref[source].astype(jnp.float32).reshape(HH, HD, BLK) * fade[:, None, :]

    weighted = share(me, part)
    for p in sources:
        remote(part.at[p], parts.at[p], part_sems.at[0, p], part_sems.at[1, p], (row, p)).wait_recv()
        weighted = weighted + share(p, parts)
    normed = weighted / tot[:, None, :]
    dots = jnp.sum(grad * normed, axis=1)
    logs[me] = jnp.concatenate([top + jnp.log(tot) * LOG2E, dots], axis=0)
    for p in peers:
        copy = remote(logs.at[me], logs.at[me], log_sems.at[0, p], log_sems.at[1, me], (row, p))
        copy.start()
        sends.append(copy)
    own = normed.reshape(HALF, BLK).T.astype(jnp.bfloat16)
    swap_halves(own, att, got, mine, swap_sems.at[0], swap_sems.at[1], row, me)()
    for p in sources:
        remote(logs.at[p], logs.at[p], log_sems.at[0, p], log_sems.at[1, p], (row, p)).wait_recv()
    for copy in sends:
        copy.wait_send()


def backward_kernel(
    key_blocks, cells, count, q_ref, g_ref, k_ref, v_ref, kt_ref, logs, dq, dk, dv, qbd, gbd, dq_acc, dk_acc, dv_acc
):
    block_diagonal((q_ref, g_ref), (qbd, gbd))
    dq_acc[...] = jnp.zeros_like(dq_acc)
    dk_acc[...] = jnp.zeros_like(dk_acc)
    dv_acc[...] = jnp.zeros_like(dv_acc)

    def pair(j, carry):
        cell = cells[0, j]
        qb = cell // key_blocks
        q_at = pl.ds(pl.multiple_of(qb * BLK, BLK), BLK)
        k_at = pl.ds(pl.multiple_of(cell % key_blocks * BLK, BLK), BLK)
        scores = dot_nt(k_ref[k_at, :], qbd[qb])
        dprob = dot_nt(v_ref[k_at, :], gbd[qb])
        low, high = logs[2 * qb], logs[2 * qb + 1]
        all_weights, all_dscore = [], []
        for h in range(H):
            lanes = slice(h * BLK, (h + 1) * BLK)
            info, r = (low, h) if h < HH else (high, h - HH)
            weights = jnp.exp2(scores[:, lanes] * SCALE2 - info[r : r + 1])
            dscore = weights * (dprob[:, lanes] - info[HH + r : HH + r + 1])
            dscore = dscore.astype(jnp.bfloat16)
            all_weights.append(weights.astype(jnp.bfloat16))
            all_dscore.append(dscore)
            at = slice(h * HD, (h + 1) * HD)
            dq_acc[at, q_at] += dot(kt_ref[at, k_at], dscore)
        dv_acc[k_at, :] += dot(jnp.concatenate(all_weights, axis=1), gbd[qb])
        dk_acc[k_at, :] += dot(jnp.concatenate(all_dscore, axis=1), qbd[qb])
        return carry

    lax.fori_loop(0, count[0, 0], pair, 0)
    for b in range(qbd.shape[0]):
        for half in range(2):
            tile = dq_acc[half * HALF : (half + 1) * HALF, b * BLK : (b + 1) * BLK]
            dq[2 * b + half] = (tile * SCALE).astype(jnp.bfloat16)

    def finish(b, carry):
        at = pl.ds(pl.multiple_of(b * BLK, BLK), BLK)
        dk[at, :] = (dk_acc[at, :] * SCALE).astype(jnp.bfloat16)
        dv[at, :] = dv_acc[at, :].astype(jnp.bfloat16)
        return carry

    lax.fori_loop(0, dk.shape[0] // BLK, finish, 0)


def reduce_kernel(
    n_col, n_z, dq, dk, dv, out_q, out_k, out_v, parts, mine, got, pair, up_out, up_in, down_out, down_in,
    part_sems, pair_sems, swap_sems, up_sems, down_sems
):
    row, me = lax.axis_index("row"), lax.axis_index("col")
    z, core = row // 2, lax.rem(row, 2)
    sibling = (row + 1 - 2 * core, me)
    above = (lax.rem(z + 1, n_z) * 2 + core, me)
    below = (lax.rem(z + n_z - 1, n_z) * 2 + core, me)
    peers, sources = others(me, n_col), senders(me, n_col)
    ring = [above, below] if n_z > 2 else [above]
    meet([sibling] + ring + [(row, p) for p in peers])
    grads = (dk, dv)
    sends = []
    for i, src in enumerate(grads):
        copy = remote(src.at[:, 1 - core], pair.at[i], pair_sems.at[0, i], pair_sems.at[1, i], sibling)
        copy.start()
        sends.append(copy)
    for p in peers:
        copy = remote(dq.at[p], parts.at[me], part_sems.at[0, p], part_sems.at[1, me], (row, p))
        copy.start()
        sends.append(copy)
    for i, src in enumerate(grads):
        sends[i].wait_recv()

    def own(i, chunk):
        return grads[i][chunk, core].astype(jnp.float32) + pair[i, chunk].astype(jnp.float32)

    n_up, n_down = n_z // 2, n_z - 1 - n_z // 2
    directions = (
        (n_up, up_out, up_in, up_sems, above, below),
        (n_down, down_out, down_in, down_sems, below, above),
    )

    def arrived(i, step, direction):
        _, out, into, sems, to, _ = direction
        remote(
            out.at[i, step], into.at[i, step], sems.at[0, i, step], sems.at[1, i, step], to
        ).wait_recv()
        return into[i, step].astype(jnp.float32)

    for step in range(n_up):
        for i in range(2):
            for d, direction in enumerate(directions):
                hops, out, into, sems, to, _ = direction
                if step >= hops:
                    continue
                away = hops - step
                chunk = lax.rem(z + (away if d == 0 else n_z - away), n_z)
                value = own(i, chunk)
                if step:
                    value = value + arrived(i, step - 1, direction)
                out[i, step] = value.astype(jnp.bfloat16)
                copy = remote(
                    out.at[i, step], into.at[i, step], sems.at[0, i, step], sems.at[1, i, step], to
                )
                copy.start()
                sends.append(copy)
        if step == n_up // 2:
            total = dq[me].astype(jnp.float32)
            for p in sources:
                remote(
                    dq.at[p], parts.at[p], part_sems.at[0, p], part_sems.at[1, p], (row, p)
                ).wait_recv()
                total = total + parts[p].astype(jnp.float32)
            finish = swap_halves(
                total.T.astype(jnp.bfloat16), out_q, got, mine, swap_sems.at[0], swap_sems.at[1], row, me
            )
    finish()
    for i, out in enumerate((out_k, out_v)):
        value = own(i, z)
        for direction in directions:
            if direction[0]:
                value = value + arrived(i, direction[0] - 1, direction)
        out[...] = value.astype(jnp.bfloat16)
    for copy in sends:
        copy.wait_send()


def shards(n_row, n_col, queries, key_lanes, values, grad_out, pattern, counts):
    bf16, f32 = jnp.bfloat16, jnp.float32
    dma = pltpu.SemaphoreType.DMA
    shape = jax.ShapeDtypeStruct
    own_q, own_g, keys, vals = queries[0], grad_out[0], key_lanes[0], values[0]
    cells, count = pattern[0], counts
    own_rows, lanes = own_q.shape[0], keys.shape[0]
    rows = own_rows * n_col
    q_blocks, key_blocks, n_z = rows // BLK, lanes // BLK, n_row // 2
    chunk = lanes // n_row

    all_q, all_g, keys_t, vals_t = call(
        functools.partial(gather_kernel, n_col),
        "gather_lanes",
        (shape((n_col, own_rows, D), bf16),) * 2 + (shape((D, lanes), bf16),) * 2,
        0,
        4,
        [dma((2, n_col)), dma((2, n_col))],
        0,
    )(own_q, own_g, keys, vals)
    all_q, all_g = all_q.reshape(rows, D), all_g.reshape(rows, D)

    part, stat = call(
        functools.partial(forward_kernel, key_blocks),
        "forward_pairs",
        (shape((n_col, HALF, BLK), bf16), shape((n_col, H, BLK), f32)),
        2,
        3,
        [
            pltpu.VMEM((q_blocks, H * BLK, D), bf16),
            pltpu.VMEM((D, rows), f32),
            pltpu.VMEM((H, rows), f32),
            pltpu.VMEM((H, rows), f32),
        ],
    )(cells, count, all_q, keys, vals_t)

    attended, logs = call(
        functools.partial(combine_kernel, n_col),
        "combine_rows",
        (shape((own_rows, D), bf16), shape((n_col, H, BLK), f32)),
        0,
        3,
        [
            pltpu.VMEM((n_col, HALF, BLK), bf16),
            pltpu.VMEM((n_col, H, BLK), f32),
            pltpu.VMEM((BLK, HALF), bf16),
            pltpu.VMEM((own_rows, HALF), bf16),
            dma((2, n_col)),
            dma((2, n_col)),
            dma((2, n_col)),
            dma((2,)),
        ],
        1,
    )(part, stat, all_g)

    dq, dk, dv = call(
        functools.partial(backward_kernel, key_blocks),
        "backward_pairs",
        (shape((n_col, HALF, BLK), bf16), shape((lanes, D), bf16), shape((lanes, D), bf16)),
        2,
        6,
        [
            pltpu.VMEM((q_blocks, H * BLK, D), bf16),
            pltpu.VMEM((q_blocks, H * BLK, D), bf16),
            pltpu.VMEM((D, rows), f32),
            pltpu.VMEM((lanes, D), f32),
            pltpu.VMEM((lanes, D), f32),
        ],
    )(cells, count, all_q, all_g, keys, vals, keys_t, logs)

    n_up = n_z // 2
    n_down = max(1, n_z - 1 - n_up)
    grad_q, grad_k, grad_v = call(
        functools.partial(reduce_kernel, n_col, n_z),
        "reduce_gradients",
        (shape((own_rows, D), bf16), shape((chunk, D), bf16), shape((chunk, D), bf16)),
        0,
        3,
        [
            pltpu.VMEM((n_col, HALF, BLK), bf16),
            pltpu.VMEM((BLK, HALF), bf16),
            pltpu.VMEM((own_rows, HALF), bf16),
            pltpu.VMEM((2, n_z, chunk, D), bf16),
            pltpu.VMEM((2, n_up, chunk, D), bf16),
            pltpu.VMEM((2, n_up, chunk, D), bf16),
            pltpu.VMEM((2, n_down, chunk, D), bf16),
            pltpu.VMEM((2, n_down, chunk, D), bf16),
            dma((2, n_col)),
            dma((2, 2)),
            dma((2,)),
            dma((2, 2, n_up)),
            dma((2, 2, n_down)),
        ],
        2,
    )(dq, dk.reshape(n_z, 2, chunk, D), dv.reshape(n_z, 2, chunk, D))
    return attended[None], grad_q[None], grad_k[None], grad_v[None]


def solution(mesh):
    return jax.shard_map(
        functools.partial(shards, mesh.shape["row"], mesh.shape["col"]),
        mesh=mesh,
        in_specs=(
            P("row", "col", None),
            P("col", None, None),
            P("col", None, None),
            P("row", "col", None),
            P("row", "col", None),
            P("row", "col"),
        ),
        out_specs=(
            P("row", "col", None),
            P("row", "col", None),
            P("col", "row", None),
            P("col", "row", None),
        ),
        check_vma=False,
    )
```

```python
import functools
import math

import jax
import jax.numpy as jnp
from jax import lax
from jax.experimental import pallas as pl
from jax.experimental.pallas import tpu as pltpu
from jax.sharding import PartitionSpec as P

D = 256
H = 8
HD = 32
BLK = 128
HALF = D // 2
HH = H // 2
NX = 4
TOGETHER = 4
MESH = pl.DeviceIdType.MESH
SCALE = 1.0 / math.sqrt(HD)
LOG2E = math.log2(math.e)
SCALE2 = SCALE * LOG2E
NEG = -1e30
VMEM_LIMIT = 56 * 1024 * 1024

vmem = pl.BlockSpec(memory_space=pltpu.VMEM)
smem = pl.BlockSpec(memory_space=pltpu.SMEM)


def call(kernel, name, out_shape, n_smem, n_vmem, scratch, collective_id=None):
    return pl.pallas_call(
        kernel,
        name=name,
        out_shape=out_shape,
        in_specs=[smem] * n_smem + [vmem] * n_vmem,
        out_specs=jax.tree.map(lambda _: vmem, out_shape),
        scratch_shapes=scratch,
        compiler_params=pltpu.CompilerParams(
            collective_id=collective_id,
            has_side_effects=collective_id is not None,
            vmem_limit_bytes=VMEM_LIMIT,
        ),
    )


def meet(peers):
    barrier = pltpu.get_barrier_semaphore()
    for peer in peers:
        pl.semaphore_signal(barrier, inc=1, device_id=peer, device_id_type=MESH)
    pl.semaphore_wait(barrier, len(peers))


def remote(src, dst, send_sem, recv_sem, device):
    return pltpu.make_async_remote_copy(
        src_ref=src,
        dst_ref=dst,
        send_sem=send_sem,
        recv_sem=recv_sem,
        device_id=device,
        device_id_type=MESH,
    )


def others(me, n):
    return [lax.rem(me + k, n) for k in range(1, n)]


def block_diagonal(pairs):
    blocks = pairs[0][1].shape[0] - 1
    lane = lax.broadcasted_iota(jnp.int32, (BLK, HALF), 1)
    masks = [
        jnp.where((lane >= h * HD) & (lane < (h + 1) * HD), 1.0, 0.0).astype(jnp.bfloat16)
        for h in range(HH)
    ]

    def one(b, carry):
        rows = pl.ds(pl.multiple_of(b * BLK, BLK), BLK)
        for ref, out in pairs:
            block = ref[rows, :]
            for h in range(HH):
                out[b, h * BLK : (h + 1) * BLK, :] = block * masks[h]
        return carry

    lax.fori_loop(0, blocks, one, 0)
    for _, out in pairs:
        out[blocks] = jnp.zeros(out.shape[1:], out.dtype)


def interleave(a, b):
    low = lax.broadcasted_iota(jnp.int32, a.shape, 1) < BLK // 2
    turned_a, turned_b = pltpu.roll(a, BLK // 2, 1), pltpu.roll(b, BLK // 2, 1)
    return jnp.where(low, a, turned_b), jnp.where(low, turned_a, b)


def dot_nt(a, b):
    return lax.dot_general(a, b, (((1,), (1,)), ((), ())), preferred_element_type=jnp.float32)


def dot(a, b):
    return jnp.dot(a, b, preferred_element_type=jnp.float32)


def half_at(h):
    return pl.ds(pl.multiple_of(h * HALF, HALF), HALF)


def gather_kernel(
    n_col, q_ref, g_ref, k_ref, v_ref, cells, count, qo, go, kh, vh, kt, vt, gt, info, swap_sems, sems
):
    row, me = lax.axis_index("row"), lax.axis_index("col")
    h, y, x = lax.rem(row, 2), me // NX, lax.rem(me, NX)
    ny = n_col // NX
    sibling = (row + 1 - 2 * h, me)
    along_x = [(row, y * NX + p) for p in others(x, NX)]
    along_y = [(row, p * NX + x) for p in others(y, ny)]
    meet([sibling] + along_x + along_y)
    info[h] = jnp.zeros(info.shape[1:], info.dtype)
    info[h, 0:1, 0 : cells.shape[1]] = cells[...]
    info[h, 1:2, 0:1] = count[...]
    swaps = [
        remote(src, dst, swap_sems.at[0, i], swap_sems.at[1, i], sibling)
        for i, (src, dst) in enumerate(
            (
                (q_ref.at[:, half_at(1 - h)], qo.at[h, y, x]),
                (g_ref.at[:, half_at(1 - h)], go.at[h, y, x]),
                (info.at[h], info.at[h]),
            )
        )
    ]
    for copy in swaps:
        copy.start()
    qo[h, y, x] = q_ref[:, half_at(h)]
    go[h, y, x] = g_ref[:, half_at(h)]

    def send(i, ref, peers):
        for p in peers:
            remote(ref, ref, sems.at[0, i], sems.at[1, i], p).start()

    def all_of(i, ref):
        return remote(ref, ref, sems.at[0, i], sems.at[1, i], sibling)

    def turn(src, out, turned):
        def one(b, carry):
            rows = pl.ds(pl.multiple_of(b * BLK, BLK), BLK)
            block = src[rows, half_at(h)]
            out[rows, :] = block
            turned[:, rows] = block.T
            return carry

        lax.fori_loop(0, src.shape[0] // BLK, one, 0)

    swaps[0].wait_recv()
    send(0, qo.at[:, y, x], along_x)
    swaps[1].wait_recv()
    send(1, go.at[:, y, x], along_y)
    gt[...] = go[:, y, x].reshape(BLK, HALF).T
    turn(k_ref, kh, kt)
    phases = [qo.at[:, y, 0 : NX - 1], go.at[:, 0 : ny - 1, x], qo.at[:, 0 : ny - 1], go.at[:, :, 0 : NX - 1]]
    all_of(0, phases[0]).wait_recv()
    send(2, qo.at[:, y], along_y)
    all_of(1, phases[1]).wait_recv()
    send(3, go.at[:, :, x], along_x)
    turn(v_ref, vh, vt)
    all_of(2, phases[2]).wait_recv()
    all_of(3, phases[3]).wait_recv()
    swaps[2].wait_recv()
    for i, ref in enumerate(phases):
        all_of(i, ref).wait_send()
    for copy in swaps:
        copy.wait_send()


def each_pair(info, key_blocks, q_blocks, together, visit):
    n_first = info[0, 1, 0]
    n_pairs = n_first + info[1, 1, 0]

    def group(i, carry):
        found = []
        for u in range(together):
            j = i * together + u
            second = (j >= n_first).astype(jnp.int32)
            real = j < n_pairs
            cell = info[second, 0, jnp.where(real, j - second * n_first, 0)]
            block = jnp.where(real, cell // key_blocks + second * q_blocks, 2 * q_blocks)
            q_at = pl.ds(pl.multiple_of(block * BLK, BLK), BLK)
            k_at = pl.ds(pl.multiple_of(cell % key_blocks * BLK, BLK), BLK)
            found.append((block, q_at, k_at))
        visit(found)
        return carry

    lax.fori_loop(0, (n_pairs + together - 1) // together, group, 0)


def head(h):
    return slice(h * BLK, (h + 1) * BLK), slice(h * HD, (h + 1) * HD)


def forward_kernel(key_blocks, info, q_ref, k_ref, vt_ref, part, stat, qbd, acc, top, tot):
    blocks = qbd.shape[0] - 1
    block_diagonal(((q_ref, qbd),))
    acc[...] = jnp.zeros_like(acc)
    tot[...] = jnp.zeros_like(tot)
    top[...] = jnp.full_like(top, NEG)

    def visit(pairs):
        scores = [dot_nt(k_ref[k_at, :], qbd[block]) for block, _, k_at in pairs]
        probs, fades, sums = [], [], []
        for (_, q_at, _), score in zip(pairs, scores):
            best = [jnp.max(score[:, head(h)[0]], axis=0, keepdims=True) for h in range(HH)]
            old = top[:, q_at]
            new = jnp.maximum(old, jnp.concatenate(best, axis=0) * SCALE2)
            top[:, q_at] = new
            fades.append(jnp.exp2(old - new))
            prob = [jnp.exp2(score[:, head(h)[0]] * SCALE2 - new[h : h + 1]) for h in range(HH)]
            sums.append([jnp.sum(p, axis=0, keepdims=True) for p in prob])
            probs.append([p.astype(jnp.bfloat16) for p in prob])
        mixed = [
            [dot(vt_ref[head(h)[1], k_at], prob[h]) for h in range(HH)]
            for (_, _, k_at), prob in zip(pairs, probs)
        ]
        for (_, q_at, _), fade, total, mix in zip(pairs, fades, sums, mixed):
            tot[:, q_at] = tot[:, q_at] * fade + jnp.concatenate(total, axis=0)
            for h in range(HH):
                at = head(h)[1]
                acc[at, q_at] = acc[at, q_at] * fade[h : h + 1] + mix[h]

    each_pair(info, key_blocks, blocks // 2, TOGETHER, visit)
    for b in range(blocks // 2):
        first = slice(b * BLK, (b + 1) * BLK)
        second = slice((b + blocks // 2) * BLK, (b + blocks // 2 + 1) * BLK)
        low, high = interleave(acc[:, first], acc[:, second])
        part[2 * b] = low.astype(jnp.bfloat16)
        part[2 * b + 1] = high.astype(jnp.bfloat16)
        stat[2 * b], stat[2 * b + 1] = interleave(
            jnp.concatenate([top[:, first], tot[:, first]], axis=0),
            jnp.concatenate([top[:, second], tot[:, second]], axis=0),
        )


def swap_rows(tile, out, mine, got, sems, h, sibling):
    rows = BLK // 2
    mine[...] = tile.astype(mine.dtype)
    copy = remote(
        mine.at[pl.ds(pl.multiple_of((1 - h) * rows, rows), rows)], got, sems.at[0], sems.at[1], sibling
    )
    copy.start()

    def finish():
        out[:, half_at(h)] = mine[pl.ds(pl.multiple_of(h * rows, rows), rows), :]
        copy.wait_recv()
        out[:, half_at(1 - h)] = got[...]
        copy.wait_send()

    return finish


def combine_kernel(n, part, stat, gt, att, logs, parts, stats, mine, got, sems, swap_sems):
    row, me = lax.axis_index("row"), lax.axis_index("col")
    h = lax.rem(row, 2)
    sibling = (row + 1 - 2 * h, me)
    peers = others(me, n)
    meet([sibling] + [(row, p) for p in peers])

    def send(i, src, dst, p):
        remote(src, dst, sems.at[0, i], sems.at[1, i], (row, p)).start()

    def all_of(i, ref):
        ref = ref.at[0 : n - 1]
        return remote(ref, ref, sems.at[0, i], sems.at[1, i], sibling)

    for p in peers:
        send(0, stat.at[p], stats.at[me], p)
    for p in peers:
        send(1, part.at[p], parts.at[me], p)
    grad = gt[...].astype(jnp.float32).reshape(HH, HD, BLK)
    stats[me] = stat[me]
    parts[me] = part[me]
    all_of(0, stats).wait_recv()
    every = stats[...]
    top = jnp.max(every[:, :HH], axis=0)
    fade = jnp.exp2(every[:, :HH] - top[None])
    tot = jnp.sum(every[:, HH:] * fade, axis=0)
    fade = fade / tot[None]
    all_of(1, parts).wait_recv()
    normed = jnp.zeros((HH, HD, BLK), jnp.float32)
    for p in range(n):
        normed = normed + parts[p].astype(jnp.float32).reshape(HH, HD, BLK) * fade[p][:, None, :]
    dots = jnp.sum(grad * normed, axis=1)
    logs[me] = jnp.concatenate([top + jnp.log(tot) * LOG2E, dots], axis=0)
    for p in peers:
        send(2, logs.at[me], logs.at[me], p)
    finish = swap_rows(normed.reshape(HALF, BLK).T, att, mine, got, swap_sems, h, sibling)
    all_of(0, stats).wait_send()
    all_of(1, parts).wait_send()
    finish()
    all_of(2, logs).wait_recv()
    all_of(2, logs).wait_send()


def backward_kernel(
    key_blocks, info, q_ref, g_ref, k_ref, v_ref, kt_ref, logs, att_in,
    dq, dkv, att, qbd, gbd, turned, dq_acc, dk_acc, dv_acc
):
    blocks = qbd.shape[0] - 1
    att[...] = att_in[...]
    block_diagonal(((q_ref, qbd), (g_ref, gbd)))
    dq_acc[...] = jnp.zeros_like(dq_acc)
    dk_acc[...] = jnp.zeros_like(dk_acc)
    dv_acc[...] = jnp.zeros_like(dv_acc)
    turned[blocks] = jnp.zeros(turned.shape[1:], turned.dtype)
    for b in range(blocks // 2):
        turned[b], turned[b + blocks // 2] = interleave(logs[2 * b], logs[2 * b + 1])

    def visit(pairs):
        scores = [dot_nt(k_ref[k_at, :], qbd[block]) for block, _, k_at in pairs]
        dprobs = [dot_nt(v_ref[k_at, :], gbd[block]) for block, _, k_at in pairs]
        all_weights, all_dscore = [], []
        for (block, _, _), score, dprob in zip(pairs, scores, dprobs):
            log = turned[block]
            weights, dscore = [], []
            for h in range(HH):
                lanes = head(h)[0]
                w = jnp.exp2(score[:, lanes] * SCALE2 - log[h : h + 1])
                d = w * (dprob[:, lanes] - log[HH + h : HH + h + 1])
                weights.append(w.astype(jnp.bfloat16))
                dscore.append(d.astype(jnp.bfloat16))
            all_weights.append(weights)
            all_dscore.append(dscore)
        new_v = [
            dot(jnp.concatenate(weights, axis=1), gbd[block])
            for (block, _, _), weights in zip(pairs, all_weights)
        ]
        new_k = [
            dot(jnp.concatenate(dscore, axis=1), qbd[block])
            for (block, _, _), dscore in zip(pairs, all_dscore)
        ]
        new_q = [
            [dot(kt_ref[head(h)[1], k_at], dscore[h]) for h in range(HH)]
            for (_, _, k_at), dscore in zip(pairs, all_dscore)
        ]
        for (_, q_at, k_at), vs, ks, qs in zip(pairs, new_v, new_k, new_q):
            dv_acc[k_at, :] += vs
            dk_acc[k_at, :] += ks
            for h in range(HH):
                dq_acc[head(h)[1], q_at] += qs[h]

    each_pair(info, key_blocks, blocks // 2, TOGETHER, visit)
    for b in range(blocks // 2):
        first = slice(b * BLK, (b + 1) * BLK)
        second = slice((b + blocks // 2) * BLK, (b + blocks // 2 + 1) * BLK)
        low, high = interleave(dq_acc[:, first] * SCALE, dq_acc[:, second] * SCALE)
        dq[2 * b // NX, 2 * b % NX] = low.astype(jnp.bfloat16)
        dq[(2 * b + 1) // NX, (2 * b + 1) % NX] = high.astype(jnp.bfloat16)

    def finish(b, carry):
        at = pl.ds(pl.multiple_of(b * BLK, BLK), BLK)
        dkv[b, 0] = (dk_acc[at, :] * SCALE).astype(jnp.bfloat16)
        dkv[b, 1] = dv_acc[at, :].astype(jnp.bfloat16)
        return carry

    lax.fori_loop(0, dkv.shape[0], finish, 0)


def chains(n):
    up, down = n // 2, n - 1 - n // 2
    found = []
    for sign, far in ((1, up), (-1, down)):
        for first in (far, far - 1):
            if first > 0:
                found.append((sign, list(range(first, 0, -2))))
    return found


def reduce_kernel(
    n_col, n_z, dq, dkv, out_q, out_k, out_v, first, middle, last, mine, got, sent, come,
    phase_sems, swap_sems, send_sem, come_sems
):
    row, me = lax.axis_index("row"), lax.axis_index("col")
    z, h, y, x = row // 2, lax.rem(row, 2), me // NX, lax.rem(me, NX)
    ny = n_col // NX
    sibling = (row + 1 - 2 * h, me)
    xs, ys = others(x, NX), others(y, ny)
    ring = chains(n_z)

    def at_z(delta):
        return (lax.rem(z + n_z + delta, n_z) * 2 + h, me)

    steps = sorted({sign * min(o, 2) for sign, senders in ring for o in senders})
    meet(
        [sibling]
        + [(row, y * NX + p) for p in xs]
        + [(row, p * NX + x) for p in ys]
        + [at_z(s) for s in sorted(set(steps + [-s for s in steps]))]
    )
    n_sent = sum(len(senders) for _, senders in ring)
    slots = {}

    def arrived(c, s):
        ref = come.at[slots[c, s]]
        remote(ref, ref, send_sem, come_sems.at[slots[c, s]], sibling).wait_recv()
        return come[slots[c, s]].astype(jnp.float32)

    def pass_on(s):
        for c, (sign, senders) in enumerate(ring):
            if s >= len(senders):
                continue
            slot = len(slots)
            slots[c, s] = slot
            target = lax.rem(z + n_z + sign * senders[s], n_z)
            if s == 0:
                src = dkv.at[target]
            else:
                src = sent.at[slot]
                sent[slot] = (dkv[target].astype(jnp.float32) + arrived(c, s - 1)).astype(jnp.bfloat16)
            remote(
                src, come.at[slot], send_sem, come_sems.at[slot], at_z(sign * min(senders[s], 2))
            ).start()

    def phase(i, ref):
        return remote(ref, ref, phase_sems.at[0, i], phase_sems.at[1, i], sibling)

    pass_on(0)
    for p in xs:
        remote(
            dq.at[:, p], first.at[x], phase_sems.at[0, 0], phase_sems.at[1, 0], (row, y * NX + p)
        ).start()
    most = max(len(senders) for _, senders in ring)
    finishes = []
    for s in range(1, max(most, 3)):
        if s < most:
            pass_on(s)
        if s == 1:
            first[x] = dq[:, x]
            phase(0, first.at[0 : NX - 1]).wait_recv()
            for b in range(ny):
                total = first[0, b].astype(jnp.float32)
                for k in range(1, NX):
                    total = total + first[k, b].astype(jnp.float32)
                middle[b] = total.astype(jnp.bfloat16)
            for p in ys:
                remote(
                    middle.at[p], last.at[y], phase_sems.at[0, 1], phase_sems.at[1, 1], (row, p * NX + x)
                ).start()
        if s == 2:
            last[y] = middle[y]
            phase(1, last.at[0 : ny - 1]).wait_recv()
            total = last[0].astype(jnp.float32)
            for k in range(1, ny):
                total = total + last[k].astype(jnp.float32)
            finishes.append(swap_rows(total.T, out_q, mine.at[0], got.at[0], swap_sems.at[0], h, sibling))
    total = dkv[z].astype(jnp.float32)
    for c, (_, senders) in enumerate(ring):
        total = total + arrived(c, len(senders) - 1)
    for i, out in enumerate((out_k, out_v)):
        finishes.append(
            swap_rows(total[i], out, mine.at[i + 1], got.at[i + 1], swap_sems.at[i + 1], h, sibling)
        )
    for finish in finishes:
        finish()
    ref = come.at[0:n_sent]
    remote(ref, ref, send_sem, come_sems.at[0], sibling).wait_send()
    phase(0, first.at[0 : NX - 1]).wait_send()
    phase(1, last.at[0 : ny - 1]).wait_send()


def leave_kernel(*refs):
    half = len(refs) // 2
    for src, dst in zip(refs[:half], refs[half:]):
        dst[0] = src[...]


def fwd_scratch(blocks):
    bf16, f32 = jnp.bfloat16, jnp.float32
    rows = blocks * BLK
    return [
        pltpu.VMEM((blocks + 1, HH * BLK, HALF), bf16),
        pltpu.VMEM((HALF, rows + BLK), f32),
        pltpu.VMEM((HH, rows + BLK), f32),
        pltpu.VMEM((HH, rows + BLK), f32),
    ]


def bwd_scratch(blocks, lanes):
    bf16, f32 = jnp.bfloat16, jnp.float32
    rows = blocks * BLK
    return [
        pltpu.VMEM((blocks + 1, HH * BLK, HALF), bf16),
        pltpu.VMEM((blocks + 1, HH * BLK, HALF), bf16),
        pltpu.VMEM((blocks + 1, H, BLK), f32),
        pltpu.VMEM((HALF, rows + BLK), f32),
        pltpu.VMEM((lanes, HALF), f32),
        pltpu.VMEM((lanes, HALF), f32),
    ]


def shards(n_row, n_col, queries, key_lanes, values, grad_out, pattern, counts):
    bf16, f32 = jnp.bfloat16, jnp.float32
    dma = pltpu.SemaphoreType.DMA
    shape = jax.ShapeDtypeStruct
    own_q, own_g, keys, vals = queries[0], grad_out[0], key_lanes[0], values[0]
    own_rows, lanes = own_q.shape[0], keys.shape[0]
    rows = own_rows * n_col * 2
    blocks, key_blocks, n_z, ny = rows // BLK, lanes // BLK, n_row // 2, n_col // NX

    all_q, all_g, kh, vh, kt, vt, gt, info = call(
        functools.partial(gather_kernel, n_col),
        "gather_lanes",
        (shape((2, ny, NX, own_rows, HALF), bf16),) * 2
        + (shape((lanes, HALF), bf16),) * 2
        + (shape((HALF, lanes), bf16),) * 2
        + (shape((HALF, BLK), bf16), shape((2, 8, BLK), jnp.int32)),
        0,
        6,
        [dma((2, 3)), dma((2, 4))],
        0,
    )(own_q, own_g, keys, vals, pattern[0], counts)
    all_q, all_g = all_q.reshape(rows, HALF), all_g.reshape(rows, HALF)

    part, stat = call(
        functools.partial(forward_kernel, key_blocks),
        "forward_pairs",
        (shape((n_col, HALF, BLK), bf16), shape((n_col, H, BLK), f32)),
        1,
        3,
        fwd_scratch(blocks),
    )(info, all_q, kh, vt)

    attended, logs = call(
        functools.partial(combine_kernel, n_col),
        "combine_rows",
        (shape((own_rows, D), bf16), shape((n_col, H, BLK), f32)),
        0,
        3,
        [
            pltpu.VMEM((n_col, HALF, BLK), bf16),
            pltpu.VMEM((n_col, H, BLK), f32),
            pltpu.VMEM((BLK, HALF), bf16),
            pltpu.VMEM((own_rows, HALF), bf16),
            dma((2, 3)),
            dma((2,)),
        ],
        1,
    )(part, stat, gt)

    dq, dkv, attended = call(
        functools.partial(backward_kernel, key_blocks),
        "backward_pairs",
        (
            shape((ny, NX, HALF, BLK), bf16),
            shape((key_blocks, 2, BLK, HALF), bf16),
            shape((own_rows, D), bf16),
        ),
        1,
        7,
        bwd_scratch(blocks, lanes),
    )(info, all_q, all_g, kh, vh, kt, logs, attended)

    n_sent = sum(len(senders) for _, senders in chains(n_z))
    grads = call(
        functools.partial(reduce_kernel, n_col, n_z),
        "reduce_gradients",
        (shape((own_rows, D), bf16),) * 3,
        0,
        2,
        [
            pltpu.VMEM((NX, ny, HALF, BLK), bf16),
            pltpu.VMEM((ny, HALF, BLK), bf16),
            pltpu.VMEM((ny, HALF, BLK), bf16),
            pltpu.VMEM((3, BLK, HALF), bf16),
            pltpu.VMEM((3, own_rows, HALF), bf16),
            pltpu.VMEM((n_sent, 2, BLK, HALF), bf16),
            pltpu.VMEM((n_sent, 2, BLK, HALF), bf16),
            dma((2, 2)),
            dma((3, 2)),
            dma,
            dma((n_sent,)),
        ],
        2,
    )(dq, dkv)
    grads = call(leave_kernel, "leave", (shape((1, own_rows, D), bf16),) * 3, 0, 3, [])(*grads)
    return (attended[None], *grads)


def solution(mesh):
    return jax.shard_map(
        functools.partial(shards, mesh.shape["row"], mesh.shape["col"]),
        mesh=mesh,
        in_specs=(
            P("row", "col", None),
            P("col", None, None),
            P("col", None, None),
            P("row", "col", None),
            P("row", "col", None),
            P("row", "col"),
        ),
        out_specs=(
            P("row", "col", None),
            P("row", "col", None),
            P("col", "row", None),
            P("col", "row", None),
        ),
        check_vma=False,
    )
```

```python
import functools
import math

import jax
import jax.numpy as jnp
from jax import lax
from jax.experimental import pallas as pl
from jax.experimental.pallas import tpu as pltpu
from jax.sharding import PartitionSpec as P

D = 256
H = 8
HD = 32
BLK = 128
HALF = D // 2
HH = H // 2
NX = 4
TOGETHER = 4
MESH = pl.DeviceIdType.MESH
SCALE = 1.0 / math.sqrt(HD)
LOG2E = math.log2(math.e)
SCALE2 = SCALE * LOG2E
NEG = -1e30
VMEM_LIMIT = 32 * 1024 * 1024

vmem = pl.BlockSpec(memory_space=pltpu.VMEM)
smem = pl.BlockSpec(memory_space=pltpu.SMEM)


def call(kernel, name, out_shape, in_specs, scratch, collective_id=None, micros=10):
    return pl.pallas_call(
        kernel,
        name=name,
        out_shape=out_shape,
        in_specs=in_specs,
        out_specs=jax.tree.map(lambda _: vmem, out_shape),
        scratch_shapes=scratch,
        cost_estimate=pl.CostEstimate(
            flops=micros * 10**9, bytes_accessed=micros * 10**6, transcendentals=0
        ),
        compiler_params=pltpu.CompilerParams(
            collective_id=collective_id,
            has_side_effects=collective_id is not None,
            vmem_limit_bytes=VMEM_LIMIT,
        ),
    )


def meet(peers):
    barrier = pltpu.get_barrier_semaphore()
    for peer in peers:
        pl.semaphore_signal(barrier, inc=1, device_id=peer, device_id_type=MESH)
    pl.semaphore_wait(barrier, len(peers))


def remote(src, dst, send_sem, recv_sem, device):
    return pltpu.make_async_remote_copy(
        src_ref=src,
        dst_ref=dst,
        send_sem=send_sem,
        recv_sem=recv_sem,
        device_id=device,
        device_id_type=MESH,
    )


def others(me, n):
    return [lax.rem(me + k, n) for k in range(1, n)]


def block_diagonal(pairs):
    blocks = pairs[0][1].shape[0] - 1
    lane = lax.broadcasted_iota(jnp.int32, (BLK, HALF), 1)
    masks = [
        jnp.where((lane >= h * HD) & (lane < (h + 1) * HD), 1.0, 0.0).astype(jnp.bfloat16)
        for h in range(HH)
    ]

    def one(b, carry):
        rows = pl.ds(pl.multiple_of(b * BLK, BLK), BLK)
        for ref, out in pairs:
            block = ref[rows, :]
            for h in range(HH):
                out[b, h * BLK : (h + 1) * BLK, :] = block * masks[h]
        return carry

    lax.fori_loop(0, blocks, one, 0, unroll=4)
    for _, out in pairs:
        out[blocks] = jnp.zeros(out.shape[1:], out.dtype)


def interleave(a, b):
    low = lax.broadcasted_iota(jnp.int32, a.shape, 1) < BLK // 2
    turned_a, turned_b = pltpu.roll(a, BLK // 2, 1), pltpu.roll(b, BLK // 2, 1)
    return jnp.where(low, a, turned_b), jnp.where(low, turned_a, b)


def dot_nt(a, b):
    return lax.dot_general(a, b, (((1,), (1,)), ((), ())), preferred_element_type=jnp.float32)


def dot(a, b):
    return jnp.dot(a, b, preferred_element_type=jnp.float32)


def half_at(h):
    return pl.ds(pl.multiple_of(h * HALF, HALF), HALF)


def turn_blocks(src, half, out):
    def one(b, carry):
        rows = pl.ds(pl.multiple_of(b * BLK, BLK), BLK)
        out[:, rows] = src[rows, half].T
        return carry

    lax.fori_loop(0, src.shape[0] // BLK, one, 0, unroll=4)


def gather_kernel(n_col, own_ref, qo, go, info, tables, swap_sems, sems):
    row, me = lax.axis_index("row"), lax.axis_index("col")
    h, y, x = lax.rem(row, 2), me // NX, lax.rem(me, NX)
    ny = n_col // NX
    rows = qo.shape[3]
    sibling = (row + 1 - 2 * h, me)
    along_x = [(row, y * NX + p) for p in others(x, NX)]
    along_y = [(row, p * NX + x) for p in others(y, ny)]
    meet([sibling] + along_x + along_y)
    swaps = [
        remote(src, dst, swap_sems.at[0, i], swap_sems.at[1, i], sibling)
        for i, (src, dst) in enumerate(
            (
                (own_ref.at[0:rows, half_at(1 - h)], qo.at[h, y, x]),
                (own_ref.at[rows : 2 * rows, half_at(1 - h)], go.at[h, y, x]),
                (own_ref.at[2 * rows :, 0:HALF], tables.at[h]),
            )
        )
    ]
    for copy in swaps:
        copy.start()
    qo[h, y, x] = own_ref[0:rows, half_at(h)]
    go[h, y, x] = own_ref[rows : 2 * rows, half_at(h)]
    tables[h] = own_ref[2 * rows :, 0:HALF]

    def send(i, ref, peers):
        for p in peers:
            remote(ref, ref, sems.at[0, i], sems.at[1, i], p).start()

    def all_of(i, ref):
        return remote(ref, ref, sems.at[0, i], sems.at[1, i], sibling)

    phases = [qo.at[:, y, 0 : NX - 1], go.at[:, 0 : ny - 1, x], qo.at[:, 0 : ny - 1], go.at[:, :, 0 : NX - 1]]
    swaps[0].wait_recv()
    send(0, qo.at[:, y, x], along_x)
    swaps[1].wait_recv()
    send(1, go.at[:, y, x], along_y)
    swaps[2].wait_recv()
    table = tables[...].astype(jnp.float32).astype(jnp.int32)
    mark = lax.broadcasted_iota(jnp.int32, table.shape, 1) == 2
    info[...] = jnp.where(mark, h, table)
    all_of(0, phases[0]).wait_recv()
    send(2, qo.at[:, y], along_y)
    all_of(1, phases[1]).wait_recv()
    send(3, go.at[:, :, x], along_x)
    all_of(2, phases[2]).wait_recv()
    all_of(3, phases[3]).wait_recv()
    for i, ref in enumerate(phases):
        all_of(i, ref).wait_send()
    for copy in swaps:
        copy.wait_send()


def each_pair(info, key_blocks, q_blocks, together, visit):
    n_first = info[0, 1, 0]
    n_pairs = n_first + info[1, 1, 0]

    def group(i, carry):
        found = []
        for u in range(together):
            j = i * together + u
            second = (j >= n_first).astype(jnp.int32)
            real = j < n_pairs
            cell = info[second, 0, jnp.where(real, j - second * n_first, 0)]
            block = jnp.where(real, cell // key_blocks + second * q_blocks, 2 * q_blocks)
            q_at = pl.ds(pl.multiple_of(block * BLK, BLK), BLK)
            k_at = pl.ds(pl.multiple_of(cell % key_blocks * BLK, BLK), BLK)
            found.append((block, q_at, k_at))
        visit(found)
        return carry

    lax.fori_loop(0, (n_pairs + together - 1) // together, group, 0)


def head(h):
    return slice(h * BLK, (h + 1) * BLK), slice(h * HD, (h + 1) * HD)


def forward_kernel(key_blocks, info, q_ref, g_ref, k_ref, v_ref, acc, stat, vt_ref, qbd, top, tot):
    own = half_at(info[0, 2, 0])
    turn_blocks(v_ref, own, vt_ref)
    blocks = qbd.shape[0] - 1
    block_diagonal(((q_ref, qbd),))
    acc[...] = jnp.zeros_like(acc)
    tot[...] = jnp.zeros_like(tot)
    top[...] = jnp.full_like(top, NEG)

    def visit(pairs):
        scores = [dot_nt(k_ref[k_at, own], qbd[block]) for block, _, k_at in pairs]
        probs, fades, sums = [], [], []
        for (_, q_at, _), score in zip(pairs, scores):
            best = [jnp.max(score[:, head(h)[0]], axis=0, keepdims=True) for h in range(HH)]
            old = top[:, q_at]
            new = jnp.maximum(old, jnp.concatenate(best, axis=0) * SCALE2)
            top[:, q_at] = new
            fades.append(jnp.exp2(old - new))
            prob = [jnp.exp2(score[:, head(h)[0]] * SCALE2 - new[h : h + 1]) for h in range(HH)]
            sums.append([jnp.sum(p, axis=0, keepdims=True) for p in prob])
            probs.append([p.astype(jnp.bfloat16) for p in prob])
        mixed = [
            [dot(vt_ref[head(h)[1], k_at], prob[h]) for h in range(HH)]
            for (_, _, k_at), prob in zip(pairs, probs)
        ]
        for (_, q_at, _), fade, total, mix in zip(pairs, fades, sums, mixed):
            tot[:, q_at] = tot[:, q_at] * fade + jnp.concatenate(total, axis=0)
            for h in range(HH):
                at = head(h)[1]
                acc[at, q_at] = acc[at, q_at] * fade[h : h + 1] + mix[h]

    each_pair(info, key_blocks, blocks // 2, TOGETHER, visit)
    lanes = blocks // 2 * BLK
    for b in range(blocks):
        r, at = divmod(b, blocks // 2)
        from_lane, to_lane = b * BLK, at * BLK
        grad = g_ref[from_lane : from_lane + BLK, :].astype(jnp.float32).T
        dots = jnp.sum((grad * acc[:, from_lane : from_lane + BLK]).reshape(HH, HD, BLK), axis=1)
        stat[r, 0:HH, to_lane : to_lane + BLK] = top[:, from_lane : from_lane + BLK]
        stat[r, HH:H, to_lane : to_lane + BLK] = tot[:, from_lane : from_lane + BLK]
        fold, to_lane = divmod(to_lane, lanes // 2)
        stat[r, fold * HH : (fold + 1) * HH, lanes + to_lane : lanes + to_lane + BLK] = dots


def swap_rows(tile, out, mine, got, sems, h, sibling):
    rows = BLK // 2
    mine[...] = tile.astype(mine.dtype)
    copy = remote(
        mine.at[pl.ds(pl.multiple_of((1 - h) * rows, rows), rows)], got, sems.at[0], sems.at[1], sibling
    )
    copy.start()

    def finish():
        out[:, half_at(h)] = mine[pl.ds(pl.multiple_of(h * rows, rows), rows), :]
        copy.wait_recv()
        out[:, half_at(1 - h)] = got[...]
        copy.wait_send()

    return finish


def combine_kernel(n, stat, logs, got, middle, sems):
    row, me = lax.axis_index("row"), lax.axis_index("col")
    y, x = me // NX, lax.rem(me, NX)
    ny = n // NX
    lanes = stat.shape[2] * 2 // 3
    along_x = (x, NX, [(row, y * NX + p) for p in others(x, NX)])
    along_y = (y, ny, [(row, p * NX + x) for p in others(y, ny)])
    meet(along_x[2] + along_y[2])

    def start(phase, r, src):
        here, _, peers = (along_x, along_y)[phase ^ r]
        for p in peers:
            dst = got.at[phase, r, here]
            remote(src, dst, sems.at[0, phase, r], sems.at[1, phase, r], p).start()
        got[phase, r, here] = src[...]

    def all_of(phase, r):
        _, size, peers = (along_x, along_y)[phase ^ r]
        ref = got.at[phase, r, 0 : size - 1]
        return remote(ref, ref, sems.at[0, phase, r], sems.at[1, phase, r], peers[0])

    def merged(phase, r):
        size = (along_x, along_y)[phase ^ r][1]
        parts = [got[phase, r, i] for i in range(size)]
        top = functools.reduce(jnp.maximum, [part[0:HH, :lanes] for part in parts])
        tot, dots = 0.0, 0.0
        for part in parts:
            fade = jnp.exp2(part[0:HH, :lanes] - top)
            tot = tot + part[HH:H, :lanes] * fade
            fold = jnp.concatenate([fade[:, : lanes // 2], fade[:, lanes // 2 :]], axis=0)
            dots = dots + part[:, lanes:] * fold
        return top, tot, dots

    for r in range(2):
        start(0, r, stat.at[r])
    for r in range(2):
        all_of(0, r).wait_recv()
        top, tot, dots = merged(0, r)
        middle[r, 0:HH, :lanes] = top
        middle[r, HH:H, :lanes] = tot
        middle[r, :, lanes:] = dots
        start(1, r, middle.at[r])
    for r in range(2):
        all_of(1, r).wait_recv()
        top, tot, dots = merged(1, r)
        total = top + jnp.log(tot) * LOG2E
        dots = jnp.concatenate([dots[0:HH], dots[HH:H]], axis=1) / tot
        for b in range(lanes // BLK):
            at = slice(b * BLK, (b + 1) * BLK)
            logs[r * (lanes // BLK) + b, 0:HH] = total[:, at]
            logs[r * (lanes // BLK) + b, HH:H] = dots[:, at]
    for phase in range(2):
        for r in range(2):
            all_of(phase, r).wait_send()


def backward_kernel(
    key_blocks, info, q_ref, g_ref, k_ref, v_ref, logs_ref, weighted, stat,
    tiles, dkv, kt_ref, qbd, gbd, logs, dq_acc, dk_acc, dv_acc
):
    blocks = qbd.shape[0] - 1
    own = half_at(info[0, 2, 0])
    turn_blocks(k_ref, own, kt_ref)
    block_diagonal(((q_ref, qbd), (g_ref, gbd)))
    dq_acc[...] = jnp.zeros_like(dq_acc)
    dk_acc[...] = jnp.zeros_like(dk_acc)
    dv_acc[...] = jnp.zeros_like(dv_acc)
    logs[0:blocks] = logs_ref[...]
    logs[blocks] = jnp.zeros(logs.shape[1:], logs.dtype)

    def visit(pairs):
        scores = [dot_nt(k_ref[k_at, own], qbd[block]) for block, _, k_at in pairs]
        dprobs = [dot_nt(v_ref[k_at, own], gbd[block]) for block, _, k_at in pairs]
        all_weights, all_dscore = [], []
        for (block, _, _), score, dprob in zip(pairs, scores, dprobs):
            log = logs[block]
            weights, dscore = [], []
            for h in range(HH):
                lanes = head(h)[0]
                w = jnp.exp2(score[:, lanes] * SCALE2 - log[h : h + 1])
                d = w * (dprob[:, lanes] - log[HH + h : HH + h + 1])
                weights.append(w.astype(jnp.bfloat16))
                dscore.append(d.astype(jnp.bfloat16))
            all_weights.append(weights)
            all_dscore.append(dscore)
        new_v = [
            dot(jnp.concatenate(weights, axis=1), gbd[block])
            for (block, _, _), weights in zip(pairs, all_weights)
        ]
        new_k = [
            dot(jnp.concatenate(dscore, axis=1), qbd[block])
            for (block, _, _), dscore in zip(pairs, all_dscore)
        ]
        new_q = [
            [dot(kt_ref[head(h)[1], k_at], dscore[h]) for h in range(HH)]
            for (_, _, k_at), dscore in zip(pairs, all_dscore)
        ]
        for (_, q_at, k_at), vs, ks, qs in zip(pairs, new_v, new_k, new_q):
            dv_acc[k_at, :] += vs
            dk_acc[k_at, :] += ks
            for h in range(HH):
                dq_acc[head(h)[1], q_at] += qs[h]

    each_pair(info, key_blocks, blocks // 2, TOGETHER, visit)
    for b in range(blocks // 2):
        at = slice(b * BLK, (b + 1) * BLK)
        grads, normed = [], []
        for r in range(2):
            block = r * (blocks // 2) + b
            lanes = slice(block * BLK, (block + 1) * BLK)
            grads.append(dq_acc[:, lanes] * SCALE)
            fade = jnp.exp2(stat[r, 0:HH, at] - logs[block, 0:HH])
            part = weighted[:, lanes].reshape(HH, HD, BLK) * fade[:, None, :]
            normed.append(part.reshape(HALF, BLK))
        for i, both in enumerate((grads, normed)):
            for k, tile in enumerate(interleave(*both)):
                tiles[i, (2 * b + k) // NX, (2 * b + k) % NX] = tile.astype(jnp.bfloat16)

    def finish(b, carry):
        at = pl.ds(pl.multiple_of(b * BLK, BLK), BLK)
        dkv[b, 0] = (dk_acc[at, :] * SCALE).astype(jnp.bfloat16)
        dkv[b, 1] = dv_acc[at, :].astype(jnp.bfloat16)
        return carry

    lax.fori_loop(0, dkv.shape[0], finish, 0, unroll=4)


def chains(n):
    up, down = n // 2, n - 1 - n // 2
    near = (up + 1) // 2
    found = []
    for first, last in ((near, 1), (up, near + 1)):
        for sign, far in ((1, up), (-1, down)):
            senders = list(range(min(first, far), last - 1, -1))
            if senders:
                found.append((sign, senders))
    return found


def reduce_kernel(
    n_col, n_z, tiles, dkv, out_q, out_k, out_v, out_a, first, middle, last, mine, got, sent, come, ended, beside,
    phase_sems, swap_sems, send_sem, come_sems, end_send, end_sems, beside_sems
):
    row, me = lax.axis_index("row"), lax.axis_index("col")
    z, h, y, x = row // 2, lax.rem(row, 2), me // NX, lax.rem(me, NX)
    ny = n_col // NX
    sibling = (row + 1 - 2 * h, me)
    xs, ys = others(x, NX), others(y, ny)
    ring = chains(n_z)
    hops = [
        [sign * (o - after) for o, after in zip(senders, senders[1:] + [0])] for sign, senders in ring
    ]

    def at_z(delta, core):
        return (lax.rem(z + n_z + delta, n_z) * 2 + core, me)

    def both_ways(deltas):
        return sorted({d % n_z for d in deltas} | {-d % n_z for d in deltas})

    def lanes_of(core):
        return pl.ds(pl.multiple_of(core * (BLK // 2), BLK // 2), BLK // 2)

    meet(
        [sibling]
        + [at_z(d, h) for d in both_ways([d for c in hops for d in c])]
        + [at_z(d, 1 - h) for d in both_ways([c[-1] for c in hops])]
        + [(row, y * NX + p) for p in xs]
        + [(row, p * NX + x) for p in ys]
    )
    slots = {}

    def arrived(i, c, s):
        slot = slots[c, s]
        ref = come.at[i, slot]
        remote(ref, ref, send_sem, come_sems.at[i, slot], sibling).wait_recv()
        return come[i, slot]

    def pass_on(s):
        for i in range(2):
            for c, (sign, senders) in enumerate(ring):
                if s >= len(senders):
                    continue
                target = lax.rem(z + n_z + sign * senders[s], n_z)
                if s == len(senders) - 1:
                    sent[i, c] = dkv[target, i] + arrived(i, c, s - 1) if s else dkv[target, i]
                    if i == 1:
                        for core in range(2):
                            remote(
                                sent.at[:, c, core * (BLK // 2) : (core + 1) * (BLK // 2)],
                                ended.at[c, h],
                                end_send,
                                end_sems.at[c, h],
                                at_z(hops[c][s], core),
                            ).start()
                    continue
                slot = slots.setdefault((c, s), len(slots))
                if s == 0:
                    src = dkv.at[target, i]
                else:
                    src = sent.at[i, len(ring) + slot]
                    sent[i, len(ring) + slot] = dkv[target, i] + arrived(i, c, s - 1)
                remote(
                    src, come.at[i, slot], send_sem, come_sems.at[i, slot], at_z(hops[c][s], h)
                ).start()

    along_x = (x, NX, [(p, (row, y * NX + p)) for p in xs])
    along_y = (y, ny, [(p, (row, p * NX + x)) for p in ys])

    def phase(i, step):
        size = (along_x, along_y)[i ^ step][1]
        ref = (first, last)[step].at[i, 0 : size - 1]
        return remote(ref, ref, phase_sems.at[0, i, step], phase_sems.at[1, i, step], sibling)

    def spread(i, step):
        here, size, peers = (along_x, along_y)[i ^ step]
        for p, device in peers:
            src = middle.at[i, p] if step else (tiles.at[0, :, p] if i == 0 else tiles.at[1, p])
            dst = (first, last)[step].at[i, here]
            remote(src, dst, phase_sems.at[0, i, step], phase_sems.at[1, i, step], device).start()
        if step:
            last[i, here] = middle[i, here]
        else:
            first[i, here] = tiles[0, :, x] if i == 0 else tiles[1, y]

    def summed(i, step, at):
        size = (along_x, along_y)[i ^ step][1]
        refs = [first[i, k, at] if step == 0 else last[i, k] for k in range(size)]
        return functools.reduce(jnp.add, [ref.astype(jnp.float32) for ref in refs])

    pass_on(0)
    aside = remote(dkv.at[z, :, lanes_of(1 - h)], beside, beside_sems.at[0], beside_sems.at[1], sibling)
    aside.start()
    for i in range(2):
        spread(i, 0)
    most = max(len(senders) for _, senders in ring)
    finishes = []
    for s in range(1, max(most, 4)):
        if s < most:
            pass_on(s)
        for i in range(2):
            if s == 2:
                phase(i, 0).wait_recv()
                for b in range((along_y, along_x)[i][1]):
                    middle[i, b] = summed(i, 0, b).astype(jnp.bfloat16)
                spread(i, 1)
            if s == 3:
                phase(i, 1).wait_recv()
                out = (out_q, out_a)[i]
                finishes.append(
                    swap_rows(summed(i, 1, 0).T, out, mine.at[i], got.at[i], swap_sems.at[i], h, sibling)
                )
    aside.wait_recv()
    for finish in finishes:
        finish()
    totals = [dkv[z, :, lanes_of(h)].astype(jnp.float32), beside[...].astype(jnp.float32)]
    for c in range(len(ring)):
        for k, core in enumerate((h, 1 - h)):
            ref = ended.at[c, core]
            remote(ref, ref, end_send, end_sems.at[c, core], sibling).wait_recv()
            totals[k] = totals[k] + ended[c, core].astype(jnp.float32)
    for total, core in zip(totals, (h, 1 - h)):
        out_k[:, half_at(core)] = total[0].astype(jnp.bfloat16)
        out_v[:, half_at(core)] = total[1].astype(jnp.bfloat16)
    aside.wait_send()
    remote(come, come, send_sem, come_sems.at[0, 0], sibling).wait_send()
    remote(ended, ended, end_send, end_sems.at[0, 0], sibling).wait_send()
    for i in range(2):
        for step in range(2):
            phase(i, step).wait_send()


def leave_kernel(*refs):
    half = len(refs) // 2
    for src, dst in zip(refs[:half], refs[half:]):
        dst[0] = src[...]


def fwd_scratch(blocks, lanes):
    bf16, f32 = jnp.bfloat16, jnp.float32
    rows = blocks * BLK
    return [
        pltpu.VMEM((HALF, lanes), bf16),
        pltpu.VMEM((blocks + 1, HH * BLK, HALF), bf16),
        pltpu.VMEM((HH, rows + BLK), f32),
        pltpu.VMEM((HH, rows + BLK), f32),
    ]


def bwd_scratch(blocks, lanes):
    bf16, f32 = jnp.bfloat16, jnp.float32
    rows = blocks * BLK
    return [
        pltpu.VMEM((HALF, lanes), bf16),
        pltpu.VMEM((blocks + 1, HH * BLK, HALF), bf16),
        pltpu.VMEM((blocks + 1, HH * BLK, HALF), bf16),
        pltpu.VMEM((blocks + 1, H, BLK), f32),
        pltpu.VMEM((HALF, rows + BLK), f32),
        pltpu.VMEM((lanes, HALF), f32),
        pltpu.VMEM((lanes, HALF), f32),
    ]


def shards(n_row, n_col, queries, key_lanes, values, grad_out, pattern, counts):
    bf16, f32 = jnp.bfloat16, jnp.float32
    dma = pltpu.SemaphoreType.DMA
    shape = jax.ShapeDtypeStruct
    own_q, own_g, keys, vals = queries[0], grad_out[0], key_lanes[0], values[0]
    own_rows, lanes = own_q.shape[0], keys.shape[0]
    rows = own_rows * n_col * 2
    blocks, key_blocks, n_z, ny = rows // BLK, lanes // BLK, n_row // 2, n_col // NX

    own_cells = jnp.pad(pattern[0].astype(bf16), ((0, 0), (0, D - pattern.shape[2])))
    own_count = jnp.pad(counts.astype(bf16), ((0, 14), (0, D - 1)))
    own = jnp.concatenate([own_q, own_g, own_cells, own_count], axis=0)
    all_q, all_g, info = call(
        functools.partial(gather_kernel, n_col),
        "gather_lanes",
        (shape((2, ny, NX, own_rows, HALF), bf16),) * 2 + (shape((2, 16, BLK), jnp.int32),),
        [vmem],
        [pltpu.VMEM((2, 16, HALF), bf16), dma((2, 3)), dma((2, 4))],
        0,
    )(own)
    all_q, all_g = all_q.reshape(rows, HALF), all_g.reshape(rows, HALF)

    folded = (H, rows // 2 * 3 // 2)
    weighted, stat = call(
        functools.partial(forward_kernel, key_blocks),
        "forward_pairs",
        (shape((HALF, rows + BLK), f32), shape((2, *folded), f32)),
        [smem] + [vmem] * 4,
        fwd_scratch(blocks, lanes),
    )(info, all_q, all_g, keys, vals)

    logs = call(
        functools.partial(combine_kernel, n_col),
        "combine_rows",
        shape((blocks, H, BLK), f32),
        [vmem],
        [
            pltpu.VMEM((2, 2, max(NX, ny), *folded), f32),
            pltpu.VMEM((2, *folded), f32),
            dma((2, 2, 2)),
        ],
        1,
    )(stat)

    tiles, dkv = call(
        functools.partial(backward_kernel, key_blocks),
        "backward_pairs",
        (shape((2, ny, NX, HALF, BLK), bf16), shape((key_blocks, 2, BLK, HALF), bf16)),
        [smem] + [vmem] * 7,
        bwd_scratch(blocks, lanes),
    )(info, all_q, all_g, keys, vals, logs, weighted, stat)

    side = max(NX, ny)
    n_chains, n_sent = len(chains(n_z)), sum(len(senders) for _, senders in chains(n_z))
    grads = call(
        functools.partial(reduce_kernel, n_col, n_z),
        "reduce_gradients",
        (shape((own_rows, D), bf16),) * 4,
        [vmem] * 2,
        [
            pltpu.VMEM((2, side, side, HALF, BLK), bf16),
            pltpu.VMEM((2, side, HALF, BLK), bf16),
            pltpu.VMEM((2, side, HALF, BLK), bf16),
            pltpu.VMEM((2, BLK, HALF), bf16),
            pltpu.VMEM((2, own_rows, HALF), bf16),
            pltpu.VMEM((2, n_sent, BLK, HALF), bf16),
            pltpu.VMEM((2, n_sent - n_chains, BLK, HALF), bf16),
            pltpu.VMEM((n_chains, 2, 2, own_rows, HALF), bf16),
            pltpu.VMEM((2, own_rows, HALF), bf16),
            dma((2, 2, 2)),
            dma((2, 2)),
            dma,
            dma((2, n_sent - n_chains)),
            dma,
            dma((n_chains, 2)),
            dma((2,)),
        ],
        2,
    )(tiles, dkv)
    grad_q, grad_k, grad_v, attended = call(
        leave_kernel, "leave", (shape((1, own_rows, D), bf16),) * 4, [vmem] * 4, []
    )(*grads)
    return attended, grad_q, grad_k, grad_v


def solution(mesh):
    return jax.shard_map(
        functools.partial(shards, mesh.shape["row"], mesh.shape["col"]),
        mesh=mesh,
        in_specs=(
            P("row", "col", None),
            P("col", None, None),
            P("col", None, None),
            P("row", "col", None),
            P("row", "col", None),
            P("row", "col"),
        ),
        out_specs=(
            P("row", "col", None),
            P("row", "col", None),
            P("col", "row", None),
            P("col", "row", None),
        ),
        check_vma=False,
    )
```

```python
import functools
import math

import jax
import jax.numpy as jnp
from jax import lax
from jax.experimental import pallas as pl
from jax.experimental.pallas import tpu as pltpu
from jax.sharding import PartitionSpec as P

D = 256
H = 8
HD = 32
BLK = 128
HALF = D // 2
HH = H // 2
NX = 4
TOGETHER = 8
GROUP = 3
MESH = pl.DeviceIdType.MESH
SCALE = 1.0 / math.sqrt(HD)
LOG2E = math.log2(math.e)
SCALE2 = SCALE * LOG2E
NEG = -1e30
VMEM_LIMIT = 32 * 1024 * 1024

vmem = pl.BlockSpec(memory_space=pltpu.VMEM)
smem = pl.BlockSpec(memory_space=pltpu.SMEM)


def call(kernel, name, out_shape, in_specs, scratch, collective_id=None, micros=10):
    return pl.pallas_call(
        kernel,
        name=name,
        out_shape=out_shape,
        in_specs=in_specs,
        out_specs=jax.tree.map(lambda _: vmem, out_shape),
        scratch_shapes=scratch,
        cost_estimate=pl.CostEstimate(
            flops=micros * 10**9, bytes_accessed=micros * 10**6, transcendentals=0
        ),
        compiler_params=pltpu.CompilerParams(
            collective_id=collective_id,
            has_side_effects=collective_id is not None,
            vmem_limit_bytes=VMEM_LIMIT,
        ),
    )


def meet(peers):
    barrier = pltpu.get_barrier_semaphore()
    for peer in peers:
        pl.semaphore_signal(barrier, inc=1, device_id=peer, device_id_type=MESH)
    pl.semaphore_wait(barrier, len(peers))


def remote(src, dst, send_sem, recv_sem, device):
    return pltpu.make_async_remote_copy(
        src_ref=src,
        dst_ref=dst,
        send_sem=send_sem,
        recv_sem=recv_sem,
        device_id=device,
        device_id_type=MESH,
    )


def others(me, n):
    return [lax.rem(me + k, n) for k in range(1, n)]


def block_diagonal(pairs):
    blocks = pairs[0][1].shape[0] - 1
    lane = lax.broadcasted_iota(jnp.int32, (BLK, HALF), 1)
    masks = [
        jnp.where((lane >= h * HD) & (lane < (h + 1) * HD), 1.0, 0.0).astype(jnp.bfloat16)
        for h in range(HH)
    ]

    def one(b, carry):
        rows = pl.ds(pl.multiple_of(b * BLK, BLK), BLK)
        for ref, out in pairs:
            block = ref[rows, :]
            for h in range(HH):
                out[b, h * BLK : (h + 1) * BLK, :] = block * masks[h]
        return carry

    lax.fori_loop(0, blocks, one, 0, unroll=4)
    for _, out in pairs:
        out[blocks] = jnp.zeros(out.shape[1:], out.dtype)


def interleave(a, b):
    low = lax.broadcasted_iota(jnp.int32, a.shape, 1) < BLK // 2
    turned_a, turned_b = pltpu.roll(a, BLK // 2, 1), pltpu.roll(b, BLK // 2, 1)
    return jnp.where(low, a, turned_b), jnp.where(low, turned_a, b)


def dot_nt(a, b):
    return lax.dot_general(a, b, (((1,), (1,)), ((), ())), preferred_element_type=jnp.float32)


def dot(a, b):
    return jnp.dot(a, b, preferred_element_type=jnp.float32)


def half_at(h):
    return pl.ds(pl.multiple_of(h * HALF, HALF), HALF)


def turn_blocks(src, half, out):
    def one(b, carry):
        rows = pl.ds(pl.multiple_of(b * BLK, BLK), BLK)
        out[:, rows] = src[rows, half].T
        return carry

    lax.fori_loop(0, src.shape[0] // BLK, one, 0, unroll=4)


def gather_kernel(n_col, own_ref, qo, go, info, tables, swap_sems, sems):
    row, me = lax.axis_index("row"), lax.axis_index("col")
    h, y, x = lax.rem(row, 2), me // NX, lax.rem(me, NX)
    ny = n_col // NX
    rows = qo.shape[3]
    sibling = (row + 1 - 2 * h, me)
    along_x = [(row, y * NX + p) for p in others(x, NX)]
    along_y = [(row, p * NX + x) for p in others(y, ny)]
    meet([sibling] + along_x + along_y)
    swaps = [
        remote(src, dst, swap_sems.at[0, i], swap_sems.at[1, i], sibling)
        for i, (src, dst) in enumerate(
            (
                (own_ref.at[0:rows, half_at(1 - h)], qo.at[h, y, x]),
                (own_ref.at[rows : 2 * rows, half_at(1 - h)], go.at[h, y, x]),
                (own_ref.at[2 * rows :, 0:HALF], tables.at[h]),
            )
        )
    ]
    for copy in swaps:
        copy.start()
    qo[h, y, x] = own_ref[0:rows, half_at(h)]
    go[h, y, x] = own_ref[rows : 2 * rows, half_at(h)]
    tables[h] = own_ref[2 * rows :, 0:HALF]

    def send(i, ref, peers):
        for p in peers:
            remote(ref, ref, sems.at[0, i], sems.at[1, i], p).start()

    def all_of(i, ref):
        return remote(ref, ref, sems.at[0, i], sems.at[1, i], sibling)

    phases = [qo.at[:, y, 0 : NX - 1], go.at[:, 0 : ny - 1, x], qo.at[:, 0 : ny - 1], go.at[:, :, 0 : NX - 1]]
    swaps[0].wait_recv()
    send(0, qo.at[:, y, x], along_x)
    swaps[1].wait_recv()
    send(1, go.at[:, y, x], along_y)
    swaps[2].wait_recv()
    table = tables[...].astype(jnp.float32).astype(jnp.int32)
    mark = lax.broadcasted_iota(jnp.int32, table.shape, 1) == 2
    info[...] = jnp.where(mark, h, table)
    all_of(0, phases[0]).wait_recv()
    send(2, qo.at[:, y], along_y)
    all_of(1, phases[1]).wait_recv()
    send(3, go.at[:, :, x], along_x)
    all_of(2, phases[2]).wait_recv()
    all_of(3, phases[3]).wait_recv()
    for i, ref in enumerate(phases):
        all_of(i, ref).wait_send()
    for copy in swaps:
        copy.wait_send()


def each_pair(info, key_blocks, q_blocks, together, visit):
    n_first = info[0, 1, 0]
    n_pairs = n_first + info[1, 1, 0]

    def group(i, carry):
        found = []
        for u in range(together):
            j = i * together + u
            second = (j >= n_first).astype(jnp.int32)
            real = j < n_pairs
            cell = info[second, 0, jnp.where(real, j - second * n_first, 0)]
            block = jnp.where(real, cell // key_blocks + second * q_blocks, 2 * q_blocks)
            q_at = pl.ds(pl.multiple_of(block * BLK, BLK), BLK)
            k_at = pl.ds(pl.multiple_of(cell % key_blocks * BLK, BLK), BLK)
            found.append((block, q_at, k_at))
        visit(found)
        return carry

    lax.fori_loop(0, (n_pairs + together - 1) // together, group, 0)


def head(h):
    return slice(h * BLK, (h + 1) * BLK), slice(h * HD, (h + 1) * HD)


def forward_kernel(key_blocks, info, q_ref, g_ref, k_ref, v_ref, acc, stat, qbd, vt_ref, top, tot):
    own = half_at(info[0, 2, 0])
    turn_blocks(v_ref, own, vt_ref)
    blocks = qbd.shape[0] - 1
    block_diagonal(((q_ref, qbd),))
    acc[...] = jnp.zeros_like(acc)
    tot[...] = jnp.zeros_like(tot)
    top[...] = jnp.full_like(top, NEG)

    def visit(pairs):
        scores = [dot_nt(k_ref[k_at, own], qbd[block]) for block, _, k_at in pairs]
        probs, fades, sums = [], [], []
        for (_, q_at, _), score in zip(pairs, scores):
            best = [jnp.max(score[:, head(h)[0]], axis=0, keepdims=True) for h in range(HH)]
            old = top[:, q_at]
            new = jnp.maximum(old, jnp.concatenate(best, axis=0) * SCALE2)
            top[:, q_at] = new
            fades.append(jnp.exp2(old - new))
            prob = [jnp.exp2(score[:, head(h)[0]] * SCALE2 - new[h : h + 1]) for h in range(HH)]
            sums.append([jnp.sum(p, axis=0, keepdims=True) for p in prob])
            probs.append([p.astype(jnp.bfloat16) for p in prob])
        mixed = [
            [dot(vt_ref[head(h)[1], k_at], prob[h]) for h in range(HH)]
            for (_, _, k_at), prob in zip(pairs, probs)
        ]
        for (_, q_at, _), fade, total, mix in zip(pairs, fades, sums, mixed):
            tot[:, q_at] = tot[:, q_at] * fade + jnp.concatenate(total, axis=0)
            for h in range(HH):
                at = head(h)[1]
                acc[at, q_at] = acc[at, q_at] * fade[h : h + 1] + mix[h]

    each_pair(info, key_blocks, blocks // 2, TOGETHER, visit)
    lanes = blocks // 2 * BLK
    for b in range(blocks):
        r, at = divmod(b, blocks // 2)
        from_lane, to_lane = b * BLK, at * BLK
        grad = g_ref[from_lane : from_lane + BLK, :].astype(jnp.float32).T
        dots = jnp.sum((grad * acc[:, from_lane : from_lane + BLK]).reshape(HH, HD, BLK), axis=1)
        stat[r, 0:HH, to_lane : to_lane + BLK] = top[:, from_lane : from_lane + BLK]
        stat[r, HH:H, to_lane : to_lane + BLK] = tot[:, from_lane : from_lane + BLK]
        fold, to_lane = divmod(to_lane, lanes // 2)
        stat[r, fold * HH : (fold + 1) * HH, lanes + to_lane : lanes + to_lane + BLK] = dots


def swap_rows(tile, out, mine, got, sems, h, sibling):
    rows = BLK // 2
    mine[...] = tile.astype(mine.dtype)
    copy = remote(
        mine.at[pl.ds(pl.multiple_of((1 - h) * rows, rows), rows)], got, sems.at[0], sems.at[1], sibling
    )
    copy.start()

    def finish():
        out[:, half_at(h)] = mine[pl.ds(pl.multiple_of(h * rows, rows), rows), :]
        copy.wait_recv()
        out[:, half_at(1 - h)] = got[...]
        copy.wait_send()

    return finish


def combine_kernel(n, stat, g_ref, k_ref, logs, gbd, kt_ref, got, middle, sems):
    row, me = lax.axis_index("row"), lax.axis_index("col")
    y, x = me // NX, lax.rem(me, NX)
    ny = n // NX
    lanes = stat.shape[2] * 2 // 3
    along_x = (x, NX, [(row, y * NX + p) for p in others(x, NX)])
    along_y = (y, ny, [(row, p * NX + x) for p in others(y, ny)])
    meet(along_x[2] + along_y[2])

    def start(phase, r, src):
        here, _, peers = (along_x, along_y)[phase ^ r]
        for p in peers:
            dst = got.at[phase, r, here]
            remote(src, dst, sems.at[0, phase, r], sems.at[1, phase, r], p).start()
        got[phase, r, here] = src[...]

    def all_of(phase, r):
        _, size, peers = (along_x, along_y)[phase ^ r]
        ref = got.at[phase, r, 0 : size - 1]
        return remote(ref, ref, sems.at[0, phase, r], sems.at[1, phase, r], peers[0])

    def merged(phase, r):
        size = (along_x, along_y)[phase ^ r][1]
        parts = [got[phase, r, i] for i in range(size)]
        top = functools.reduce(jnp.maximum, [part[0:HH, :lanes] for part in parts])
        tot, dots = 0.0, 0.0
        for part in parts:
            fade = jnp.exp2(part[0:HH, :lanes] - top)
            tot = tot + part[HH:H, :lanes] * fade
            fold = jnp.concatenate([fade[:, : lanes // 2], fade[:, lanes // 2 :]], axis=0)
            dots = dots + part[:, lanes:] * fold
        return top, tot, dots

    for r in range(2):
        start(0, r, stat.at[r])
    block_diagonal(((g_ref, gbd),))
    for r in range(2):
        all_of(0, r).wait_recv()
        top, tot, dots = merged(0, r)
        middle[r, 0:HH, :lanes] = top
        middle[r, HH:H, :lanes] = tot
        middle[r, :, lanes:] = dots
        start(1, r, middle.at[r])
    turn_blocks(k_ref, half_at(lax.rem(row, 2)), kt_ref)
    for r in range(2):
        all_of(1, r).wait_recv()
        top, tot, dots = merged(1, r)
        total = top + jnp.log(tot) * LOG2E
        dots = jnp.concatenate([dots[0:HH], dots[HH:H]], axis=1) / tot
        for b in range(lanes // BLK):
            at = slice(b * BLK, (b + 1) * BLK)
            logs[r * (lanes // BLK) + b, 0:HH] = total[:, at]
            logs[r * (lanes // BLK) + b, HH:H] = dots[:, at]
    for phase in range(2):
        for r in range(2):
            all_of(phase, r).wait_send()


def backward_kernel(
    key_blocks, info, qbd, gbd, k_ref, v_ref, kt_ref, logs_ref, weighted, stat,
    tiles, dkv, logs, dq_acc, dk_acc, dv_acc
):
    blocks = qbd.shape[0] - 1
    own = half_at(info[0, 2, 0])
    dq_acc[...] = jnp.zeros_like(dq_acc)
    dk_acc[...] = jnp.zeros_like(dk_acc)
    dv_acc[...] = jnp.zeros_like(dv_acc)
    logs[0:blocks] = logs_ref[...]
    logs[blocks] = jnp.zeros(logs.shape[1:], logs.dtype)

    def visit(pairs):
        scores = [dot_nt(k_ref[k_at, own], qbd[block]) for block, _, k_at in pairs]
        dprobs = [dot_nt(v_ref[k_at, own], gbd[block]) for block, _, k_at in pairs]
        all_weights, all_dscore = [], []
        for (block, _, _), score, dprob in zip(pairs, scores, dprobs):
            log = logs[block]
            weights, dscore = [], []
            for h in range(HH):
                lanes = head(h)[0]
                w = jnp.exp2(score[:, lanes] * SCALE2 - log[h : h + 1])
                d = w * (dprob[:, lanes] - log[HH + h : HH + h + 1])
                weights.append(w.astype(jnp.bfloat16))
                dscore.append(d.astype(jnp.bfloat16))
            all_weights.append(weights)
            all_dscore.append(dscore)
        new_v = [
            dot(jnp.concatenate(weights, axis=1), gbd[block])
            for (block, _, _), weights in zip(pairs, all_weights)
        ]
        new_k = [
            dot(jnp.concatenate(dscore, axis=1), qbd[block])
            for (block, _, _), dscore in zip(pairs, all_dscore)
        ]
        new_q = [
            [dot(kt_ref[head(h)[1], k_at], dscore[h]) for h in range(HH)]
            for (_, _, k_at), dscore in zip(pairs, all_dscore)
        ]
        for (_, q_at, k_at), vs, ks, qs in zip(pairs, new_v, new_k, new_q):
            dv_acc[k_at, :] += vs
            dk_acc[k_at, :] += ks
            for h in range(HH):
                dq_acc[head(h)[1], q_at] += qs[h]

    each_pair(info, key_blocks, blocks // 2, TOGETHER, visit)
    for b in range(blocks // 2):
        at = slice(b * BLK, (b + 1) * BLK)
        grads, normed = [], []
        for r in range(2):
            block = r * (blocks // 2) + b
            lanes = slice(block * BLK, (block + 1) * BLK)
            grads.append(dq_acc[:, lanes] * SCALE)
            fade = jnp.exp2(stat[r, 0:HH, at] - logs[block, 0:HH])
            part = weighted[:, lanes].reshape(HH, HD, BLK) * fade[:, None, :]
            normed.append(part.reshape(HALF, BLK))
        for i, both in enumerate((grads, normed)):
            for k, tile in enumerate(interleave(*both)):
                tiles[i, (2 * b + k) // NX, (2 * b + k) % NX] = tile.astype(jnp.bfloat16)

    def finish(b, carry):
        at = pl.ds(pl.multiple_of(b * BLK, BLK), BLK)
        dkv[b, 0] = (dk_acc[at, :] * SCALE).astype(jnp.bfloat16)
        dkv[b, 1] = dv_acc[at, :].astype(jnp.bfloat16)
        return carry

    lax.fori_loop(0, dkv.shape[0], finish, 0, unroll=4)


def tree(n):
    steps = []
    for sign, far in ((1, n // 2), (-1, n - 1 - n // 2)):
        depth = {}
        for o in range(far, 0, -1):
            to = max(o - GROUP, 0) if o % GROUP == 0 else o - 1
            depth[to] = max(depth.get(to, 0), depth.get(o, 0) + 1)
            steps.append((depth.get(o, 0), sign, o, to))
    return [
        [step[1:] for step in steps if step[0] == level] for level in range(max(s[0] for s in steps) + 1)
    ]


def reduce_kernel(
    n_col, n_z, tiles, dkv, out_q, out_k, out_v, out_a, first, middle, last, mine, got, sent, come, ended, beside,
    phase_sems, swap_sems, send_sem, come_sems, end_send, end_sems, beside_sems
):
    row, me = lax.axis_index("row"), lax.axis_index("col")
    z, h, y, x = row // 2, lax.rem(row, 2), me // NX, lax.rem(me, NX)
    ny = n_col // NX
    sibling = (row + 1 - 2 * h, me)
    xs, ys = others(x, NX), others(y, ny)
    levels = tree(n_z)
    edges = [edge for level in levels for edge in level]
    ends = [edge for edge in edges if edge[2] == 0]
    inner = [edge for edge in edges if edge[2] != 0]

    def at_z(delta, core):
        return (lax.rem(z + n_z + delta, n_z) * 2 + core, me)

    def both_ways(deltas):
        return sorted({d % n_z for d in deltas} | {-d % n_z for d in deltas})

    def lanes_of(core):
        return pl.ds(pl.multiple_of(core * (BLK // 2), BLK // 2), BLK // 2)

    meet(
        [sibling]
        + [at_z(d, h) for d in both_ways([sign * (o - to) for sign, o, to in edges])]
        + [at_z(d, 1 - h) for d in both_ways([sign * o for sign, o, _ in ends])]
        + [(row, y * NX + p) for p in xs]
        + [(row, p * NX + x) for p in ys]
    )

    def arrived(i, slot):
        ref = come.at[i, slot]
        remote(ref, ref, send_sem, come_sems.at[i, slot], sibling).wait_recv()
        return come[i, slot]

    def pass_on(level):
        for edge in sorted(level, key=lambda e: -e[1]):
            for i in range(2):
                sign, o, to = edge
                target = lax.rem(z + n_z + sign * o, n_z)
                src = dkv.at[target, i]
                from_slots = [k for k, e in enumerate(inner) if (e[0], e[2]) == (sign, o)]
                if from_slots or edge in ends:
                    value = dkv[target, i]
                    for k in from_slots:
                        value = value + arrived(i, k)
                    src = sent.at[i, edges.index(edge)]
                    src[...] = value
                if edge in inner:
                    slot = inner.index(edge)
                    remote(
                        src, come.at[i, slot], send_sem, come_sems.at[i, slot], at_z(sign * (o - to), h)
                    ).start()
                elif i == 1:
                    slot = ends.index(edge)
                    for core in range(2):
                        remote(
                            sent.at[:, edges.index(edge), core * (BLK // 2) : (core + 1) * (BLK // 2)],
                            ended.at[slot, h],
                            end_send,
                            end_sems.at[slot, h],
                            at_z(sign * o, core),
                        ).start()

    along_x = (x, NX, [(p, (row, y * NX + p)) for p in xs])
    along_y = (y, ny, [(p, (row, p * NX + x)) for p in ys])

    def phase(i, step):
        size = (along_x, along_y)[i ^ step][1]
        ref = (first, last)[step].at[i, 0 : size - 1]
        return remote(ref, ref, phase_sems.at[0, i, step], phase_sems.at[1, i, step], sibling)

    def spread(i, step):
        here, size, peers = (along_x, along_y)[i ^ step]
        for p, device in peers:
            src = middle.at[i, p] if step else (tiles.at[0, :, p] if i == 0 else tiles.at[1, p])
            dst = (first, last)[step].at[i, here]
            remote(src, dst, phase_sems.at[0, i, step], phase_sems.at[1, i, step], device).start()
        if step:
            last[i, here] = middle[i, here]
        else:
            first[i, here] = tiles[0, :, x] if i == 0 else tiles[1, y]

    def summed(i, step, at):
        size = (along_x, along_y)[i ^ step][1]
        refs = [first[i, k, at] if step == 0 else last[i, k] for k in range(size)]
        return functools.reduce(jnp.add, [ref.astype(jnp.float32) for ref in refs])

    pass_on(levels[0])
    aside = remote(dkv.at[z, :, lanes_of(1 - h)], beside, beside_sems.at[0], beside_sems.at[1], sibling)
    aside.start()
    for i in range(2):
        spread(i, 0)
    finishes = []
    for s in range(1, max(len(levels), 4)):
        if s < len(levels):
            pass_on(levels[s])
        for i in range(2):
            if s == 2:
                phase(i, 0).wait_recv()
                for b in range((along_y, along_x)[i][1]):
                    middle[i, b] = summed(i, 0, b).astype(jnp.bfloat16)
                spread(i, 1)
            if s == 3:
                phase(i, 1).wait_recv()
                out = (out_q, out_a)[i]
                finishes.append(
                    swap_rows(summed(i, 1, 0).T, out, mine.at[i], got.at[i], swap_sems.at[i], h, sibling)
                )
    aside.wait_recv()
    for finish in finishes:
        finish()
    totals = [dkv[z, :, lanes_of(h)].astype(jnp.float32), beside[...].astype(jnp.float32)]
    for c in range(len(ends)):
        for k, core in enumerate((h, 1 - h)):
            ref = ended.at[c, core]
            remote(ref, ref, end_send, end_sems.at[c, core], sibling).wait_recv()
            totals[k] = totals[k] + ended[c, core].astype(jnp.float32)
    for total, core in zip(totals, (h, 1 - h)):
        out_k[:, half_at(core)] = total[0].astype(jnp.bfloat16)
        out_v[:, half_at(core)] = total[1].astype(jnp.bfloat16)
    aside.wait_send()
    remote(come, come, send_sem, come_sems.at[0, 0], sibling).wait_send()
    remote(ended, ended, end_send, end_sems.at[0, 0], sibling).wait_send()
    for i in range(2):
        for step in range(2):
            phase(i, step).wait_send()


def leave_kernel(*refs):
    half = len(refs) // 2
    for src, dst in zip(refs[:half], refs[half:]):
        dst[0] = src[...]


def fwd_scratch(blocks, lanes):
    f32 = jnp.float32
    rows = blocks * BLK
    return [
        pltpu.VMEM((HALF, lanes), jnp.bfloat16),
        pltpu.VMEM((HH, rows + BLK), f32),
        pltpu.VMEM((HH, rows + BLK), f32),
    ]


def bwd_scratch(blocks, lanes):
    f32 = jnp.float32
    rows = blocks * BLK
    return [
        pltpu.VMEM((blocks + 1, H, BLK), f32),
        pltpu.VMEM((HALF, rows + BLK), f32),
        pltpu.VMEM((lanes, HALF), f32),
        pltpu.VMEM((lanes, HALF), f32),
    ]


def shards(n_row, n_col, queries, key_lanes, values, grad_out, pattern, counts):
    bf16, f32 = jnp.bfloat16, jnp.float32
    dma = pltpu.SemaphoreType.DMA
    shape = jax.ShapeDtypeStruct
    own_q, own_g, keys, vals = queries[0], grad_out[0], key_lanes[0], values[0]
    own_rows, lanes = own_q.shape[0], keys.shape[0]
    rows = own_rows * n_col * 2
    blocks, key_blocks, n_z, ny = rows // BLK, lanes // BLK, n_row // 2, n_col // NX

    own_cells = jnp.pad(pattern[0].astype(bf16), ((0, 0), (0, D - pattern.shape[2])))
    own_count = jnp.pad(counts.astype(bf16), ((0, 14), (0, D - 1)))
    own = jnp.concatenate([own_q, own_g, own_cells, own_count], axis=0)
    all_q, all_g, info = call(
        functools.partial(gather_kernel, n_col),
        "gather_lanes",
        (shape((2, ny, NX, own_rows, HALF), bf16),) * 2 + (shape((2, 16, BLK), jnp.int32),),
        [vmem],
        [pltpu.VMEM((2, 16, HALF), bf16), dma((2, 3)), dma((2, 4))],
        0,
    )(own)
    all_q, all_g = all_q.reshape(rows, HALF), all_g.reshape(rows, HALF)

    folded = (H, rows // 2 * 3 // 2)
    by_head = shape((blocks + 1, HH * BLK, HALF), bf16)
    weighted, stat, qbd = call(
        functools.partial(forward_kernel, key_blocks),
        "forward_pairs",
        (shape((HALF, rows + BLK), f32), shape((2, *folded), f32), by_head),
        [smem] + [vmem] * 4,
        fwd_scratch(blocks, lanes),
    )(info, all_q, all_g, keys, vals)

    logs, gbd, keys_t = call(
        functools.partial(combine_kernel, n_col),
        "combine_rows",
        (shape((blocks, H, BLK), f32), by_head, shape((HALF, lanes), bf16)),
        [vmem] * 3,
        [
            pltpu.VMEM((2, 2, max(NX, ny), *folded), f32),
            pltpu.VMEM((2, *folded), f32),
            dma((2, 2, 2)),
        ],
        1,
    )(stat, all_g, keys)

    tiles, dkv = call(
        functools.partial(backward_kernel, key_blocks),
        "backward_pairs",
        (shape((2, ny, NX, HALF, BLK), bf16), shape((key_blocks, 2, BLK, HALF), bf16)),
        [smem] + [vmem] * 8,
        bwd_scratch(blocks, lanes),
    )(info, qbd, gbd, keys, vals, keys_t, logs, weighted, stat)

    side = max(NX, ny)
    edges = [edge for level in tree(n_z) for edge in level]
    n_sent, n_ends = len(edges), sum(edge[2] == 0 for edge in edges)
    grads = call(
        functools.partial(reduce_kernel, n_col, n_z),
        "reduce_gradients",
        (shape((own_rows, D), bf16),) * 4,
        [vmem] * 2,
        [
            pltpu.VMEM((2, side, side, HALF, BLK), bf16),
            pltpu.VMEM((2, side, HALF, BLK), bf16),
            pltpu.VMEM((2, side, HALF, BLK), bf16),
            pltpu.VMEM((2, BLK, HALF), bf16),
            pltpu.VMEM((2, own_rows, HALF), bf16),
            pltpu.VMEM((2, n_sent, BLK, HALF), bf16),
            pltpu.VMEM((2, n_sent - n_ends, BLK, HALF), bf16),
            pltpu.VMEM((n_ends, 2, 2, own_rows, HALF), bf16),
            pltpu.VMEM((2, own_rows, HALF), bf16),
            dma((2, 2, 2)),
            dma((2, 2)),
            dma,
            dma((2, n_sent - n_ends)),
            dma,
            dma((n_ends, 2)),
            dma((2,)),
        ],
        2,
    )(tiles, dkv)
    grad_q, grad_k, grad_v, attended = call(
        leave_kernel, "leave", (shape((1, own_rows, D), bf16),) * 4, [vmem] * 4, []
    )(*grads)
    return attended, grad_q, grad_k, grad_v


def solution(mesh):
    return jax.shard_map(
        functools.partial(shards, mesh.shape["row"], mesh.shape["col"]),
        mesh=mesh,
        in_specs=(
            P("row", "col", None),
            P("col", None, None),
            P("col", None, None),
            P("row", "col", None),
            P("row", "col", None),
            P("row", "col"),
        ),
        out_specs=(
            P("row", "col", None),
            P("row", "col", None),
            P("col", "row", None),
            P("col", "row", None),
        ),
        check_vma=False,
    )
```

```python
import functools
import math

import jax
import jax.numpy as jnp
from jax import lax
from jax.experimental import pallas as pl
from jax.experimental.pallas import tpu as pltpu
from jax.sharding import PartitionSpec as P

D = 256
H = 8
HD = 32
BLK = 128
HALF = D // 2
HH = H // 2
NX = 4
TOGETHER = 8
GROUP = 3
MESH = pl.DeviceIdType.MESH
SCALE = 1.0 / math.sqrt(HD)
LOG2E = math.log2(math.e)
SCALE2 = SCALE * LOG2E
NEG = -1e30
VMEM_LIMIT = 32 * 1024 * 1024

vmem = pl.BlockSpec(memory_space=pltpu.VMEM)
smem = pl.BlockSpec(memory_space=pltpu.SMEM)


def call(kernel, name, out_shape, in_specs, scratch, collective_id=None, micros=10):
    return pl.pallas_call(
        kernel,
        name=name,
        out_shape=out_shape,
        in_specs=in_specs,
        out_specs=jax.tree.map(lambda _: vmem, out_shape),
        scratch_shapes=scratch,
        cost_estimate=pl.CostEstimate(
            flops=micros * 10**9, bytes_accessed=micros * 10**6, transcendentals=0
        ),
        compiler_params=pltpu.CompilerParams(
            collective_id=collective_id,
            has_side_effects=collective_id is not None,
            vmem_limit_bytes=VMEM_LIMIT,
        ),
    )


def meet(peers):
    barrier = pltpu.get_barrier_semaphore()
    for peer in peers:
        pl.semaphore_signal(barrier, inc=1, device_id=peer, device_id_type=MESH)
    pl.semaphore_wait(barrier, len(peers))


def remote(src, dst, send_sem, recv_sem, device):
    return pltpu.make_async_remote_copy(
        src_ref=src,
        dst_ref=dst,
        send_sem=send_sem,
        recv_sem=recv_sem,
        device_id=device,
        device_id_type=MESH,
    )


def others(me, n):
    return [lax.rem(me + k, n) for k in range(1, n)]


def block_diagonal(pairs):
    blocks = pairs[0][1].shape[0] - 1
    lane = lax.broadcasted_iota(jnp.int32, (BLK, HALF), 1)
    masks = [
        jnp.where((lane >= h * HD) & (lane < (h + 1) * HD), 1.0, 0.0).astype(jnp.bfloat16)
        for h in range(HH)
    ]

    def one(b, carry):
        rows = pl.ds(pl.multiple_of(b * BLK, BLK), BLK)
        for ref, out in pairs:
            block = ref[rows, :]
            for h in range(HH):
                out[b, h * BLK : (h + 1) * BLK, :] = block * masks[h]
        return carry

    lax.fori_loop(0, blocks, one, 0, unroll=4)
    for _, out in pairs:
        out[blocks] = jnp.zeros(out.shape[1:], out.dtype)


def interleave(a, b):
    low = lax.broadcasted_iota(jnp.int32, a.shape, 1) < BLK // 2
    turned_a, turned_b = pltpu.roll(a, BLK // 2, 1), pltpu.roll(b, BLK // 2, 1)
    return jnp.where(low, a, turned_b), jnp.where(low, turned_a, b)


def dot_nt(a, b):
    return lax.dot_general(a, b, (((1,), (1,)), ((), ())), preferred_element_type=jnp.float32)


def dot(a, b):
    return jnp.dot(a, b, preferred_element_type=jnp.float32)


def half_at(h):
    return pl.ds(pl.multiple_of(h * HALF, HALF), HALF)


def turn_blocks(src, half, out):
    def one(b, carry):
        rows = pl.ds(pl.multiple_of(b * BLK, BLK), BLK)
        out[:, rows] = src[rows, half].T
        return carry

    lax.fori_loop(0, src.shape[0] // BLK, one, 0, unroll=4)


def gather_kernel(n_col, own_ref, qo, go, info, tables, swap_sems, sems):
    row, me = lax.axis_index("row"), lax.axis_index("col")
    h, y, x = lax.rem(row, 2), me // NX, lax.rem(me, NX)
    ny = n_col // NX
    rows = qo.shape[3]
    sibling = (row + 1 - 2 * h, me)
    along_x = [(row, y * NX + p) for p in others(x, NX)]
    along_y = [(row, p * NX + x) for p in others(y, ny)]
    meet([sibling] + along_x + along_y)
    swaps = [
        remote(src, dst, swap_sems.at[0, i], swap_sems.at[1, i], sibling)
        for i, (src, dst) in enumerate(
            (
                (own_ref.at[0:rows, half_at(1 - h)], qo.at[h, y, x]),
                (own_ref.at[rows : 2 * rows, half_at(1 - h)], go.at[h, y, x]),
                (own_ref.at[2 * rows :, 0:HALF], tables.at[h]),
            )
        )
    ]
    for copy in swaps:
        copy.start()
    qo[h, y, x] = own_ref[0:rows, half_at(h)]
    go[h, y, x] = own_ref[rows : 2 * rows, half_at(h)]
    tables[h] = own_ref[2 * rows :, 0:HALF]

    def send(i, ref, peers):
        for p in peers:
            remote(ref, ref, sems.at[0, i], sems.at[1, i], p).start()

    def all_of(i, ref):
        return remote(ref, ref, sems.at[0, i], sems.at[1, i], sibling)

    phases = [qo.at[:, y, 0 : NX - 1], go.at[:, 0 : ny - 1, x], qo.at[:, 0 : ny - 1], go.at[:, :, 0 : NX - 1]]
    swaps[0].wait_recv()
    send(0, qo.at[:, y, x], along_x)
    swaps[1].wait_recv()
    send(1, go.at[:, y, x], along_y)
    swaps[2].wait_recv()
    table = tables[...].astype(jnp.float32).astype(jnp.int32)
    mark = lax.broadcasted_iota(jnp.int32, table.shape, 1) == 2
    info[...] = jnp.where(mark, h, table)
    all_of(0, phases[0]).wait_recv()
    send(2, qo.at[:, y], along_y)
    all_of(1, phases[1]).wait_recv()
    send(3, go.at[:, :, x], along_x)
    all_of(2, phases[2]).wait_recv()
    all_of(3, phases[3]).wait_recv()
    for i, ref in enumerate(phases):
        all_of(i, ref).wait_send()
    for copy in swaps:
        copy.wait_send()


def each_pair(info, key_blocks, q_blocks, together, visit):
    n_first = info[0, 1, 0]
    n_pairs = n_first + info[1, 1, 0]

    def group(i, carry):
        found = []
        for u in range(together):
            j = i * together + u
            second = (j >= n_first).astype(jnp.int32)
            real = j < n_pairs
            cell = info[second, 0, jnp.where(real, j - second * n_first, 0)]
            block = jnp.where(real, cell // key_blocks + second * q_blocks, 2 * q_blocks)
            q_at = pl.ds(pl.multiple_of(block * BLK, BLK), BLK)
            k_at = pl.ds(pl.multiple_of(cell % key_blocks * BLK, BLK), BLK)
            found.append((block, q_at, k_at))
        visit(found)
        return carry

    lax.fori_loop(0, (n_pairs + together - 1) // together, group, 0)


def head(h):
    return slice(h * BLK, (h + 1) * BLK), slice(h * HD, (h + 1) * HD)


def forward_kernel(key_blocks, info, q_ref, g_ref, k_ref, v_ref, acc, stat, qbd, vt_ref, top, tot):
    own = half_at(info[0, 2, 0])
    turn_blocks(v_ref, own, vt_ref)
    blocks = qbd.shape[0] - 1
    block_diagonal(((q_ref, qbd),))
    acc[...] = jnp.zeros_like(acc)
    tot[...] = jnp.zeros_like(tot)
    top[...] = jnp.full_like(top, NEG)

    def visit(pairs):
        scores = [dot_nt(k_ref[k_at, own], qbd[block]) for block, _, k_at in pairs]
        probs, fades, sums = [], [], []
        for (_, q_at, _), score in zip(pairs, scores):
            best = [jnp.max(score[:, head(h)[0]], axis=0, keepdims=True) for h in range(HH)]
            old = top[:, q_at]
            new = jnp.maximum(old, jnp.concatenate(best, axis=0) * SCALE2)
            top[:, q_at] = new
            fades.append(jnp.exp2(old - new))
            prob = [jnp.exp2(score[:, head(h)[0]] * SCALE2 - new[h : h + 1]) for h in range(HH)]
            sums.append([jnp.sum(p, axis=0, keepdims=True) for p in prob])
            probs.append([p.astype(jnp.bfloat16) for p in prob])
        mixed = [
            [dot(vt_ref[head(h)[1], k_at], prob[h]) for h in range(HH)]
            for (_, _, k_at), prob in zip(pairs, probs)
        ]
        for (_, q_at, _), fade, total, mix in zip(pairs, fades, sums, mixed):
            tot[:, q_at] = tot[:, q_at] * fade + jnp.concatenate(total, axis=0)
            for h in range(HH):
                at = head(h)[1]
                acc[at, q_at] = acc[at, q_at] * fade[h : h + 1] + mix[h]

    each_pair(info, key_blocks, blocks // 2, TOGETHER, visit)
    lanes = blocks // 2 * BLK
    for b in range(blocks):
        r, at = divmod(b, blocks // 2)
        from_lane, to_lane = b * BLK, at * BLK
        grad = g_ref[from_lane : from_lane + BLK, :].astype(jnp.float32).T
        dots = jnp.sum((grad * acc[:, from_lane : from_lane + BLK]).reshape(HH, HD, BLK), axis=1)
        stat[r, 0:HH, to_lane : to_lane + BLK] = top[:, from_lane : from_lane + BLK]
        stat[r, HH:H, to_lane : to_lane + BLK] = tot[:, from_lane : from_lane + BLK]
        fold, to_lane = divmod(to_lane, lanes // 2)
        stat[r, fold * HH : (fold + 1) * HH, lanes + to_lane : lanes + to_lane + BLK] = dots


def swap_rows(tile, out, mine, got, sems, h, sibling):
    rows = BLK // 2
    mine[...] = tile.astype(mine.dtype)
    copy = remote(
        mine.at[pl.ds(pl.multiple_of((1 - h) * rows, rows), rows)], got, sems.at[0], sems.at[1], sibling
    )
    copy.start()

    def finish():
        out[:, half_at(h)] = mine[pl.ds(pl.multiple_of(h * rows, rows), rows), :]
        copy.wait_recv()
        out[:, half_at(1 - h)] = got[...]
        copy.wait_send()

    return finish


def combine_kernel(n, stat, g_ref, k_ref, logs, gbd, kt_ref, got, middle, sems):
    row, me = lax.axis_index("row"), lax.axis_index("col")
    y, x = me // NX, lax.rem(me, NX)
    ny = n // NX
    lanes = stat.shape[2] * 2 // 3
    along_x = (x, NX, [(row, y * NX + p) for p in others(x, NX)])
    along_y = (y, ny, [(row, p * NX + x) for p in others(y, ny)])
    meet(along_x[2] + along_y[2])

    def start(phase, r, src):
        here, _, peers = (along_x, along_y)[phase ^ r]
        for p in peers:
            dst = got.at[phase, r, here]
            remote(src, dst, sems.at[0, phase, r], sems.at[1, phase, r], p).start()
        got[phase, r, here] = src[...]

    def all_of(phase, r):
        _, size, peers = (along_x, along_y)[phase ^ r]
        ref = got.at[phase, r, 0 : size - 1]
        return remote(ref, ref, sems.at[0, phase, r], sems.at[1, phase, r], peers[0])

    def merged(phase, r):
        size = (along_x, along_y)[phase ^ r][1]
        parts = [got[phase, r, i] for i in range(size)]
        top = functools.reduce(jnp.maximum, [part[0:HH, :lanes] for part in parts])
        tot, dots = 0.0, 0.0
        for part in parts:
            fade = jnp.exp2(part[0:HH, :lanes] - top)
            tot = tot + part[HH:H, :lanes] * fade
            fold = jnp.concatenate([fade[:, : lanes // 2], fade[:, lanes // 2 :]], axis=0)
            dots = dots + part[:, lanes:] * fold
        return top, tot, dots

    for r in range(2):
        start(0, r, stat.at[r])
    block_diagonal(((g_ref, gbd),))
    for r in range(2):
        all_of(0, r).wait_recv()
        top, tot, dots = merged(0, r)
        middle[r, 0:HH, :lanes] = top
        middle[r, HH:H, :lanes] = tot
        middle[r, :, lanes:] = dots
        start(1, r, middle.at[r])
    turn_blocks(k_ref, half_at(lax.rem(row, 2)), kt_ref)
    for r in range(2):
        all_of(1, r).wait_recv()
        top, tot, dots = merged(1, r)
        total = top + jnp.log(tot) * LOG2E
        dots = jnp.concatenate([dots[0:HH], dots[HH:H]], axis=1) / tot
        for b in range(lanes // BLK):
            at = slice(b * BLK, (b + 1) * BLK)
            logs[r * (lanes // BLK) + b, 0:HH] = total[:, at]
            logs[r * (lanes // BLK) + b, HH:H] = dots[:, at]
    for phase in range(2):
        for r in range(2):
            all_of(phase, r).wait_send()


def backward_kernel(
    key_blocks, info, qbd, gbd, k_ref, v_ref, kt_ref, logs_ref, weighted, stat,
    tiles, dkv, logs, dq_acc, dk_acc, dv_acc
):
    blocks = qbd.shape[0] - 1
    own = half_at(info[0, 2, 0])
    dq_acc[...] = jnp.zeros_like(dq_acc)
    dk_acc[...] = jnp.zeros_like(dk_acc)
    dv_acc[...] = jnp.zeros_like(dv_acc)
    logs[0:blocks] = logs_ref[...]
    logs[blocks] = jnp.zeros(logs.shape[1:], logs.dtype)

    def visit(pairs):
        scores = [dot_nt(k_ref[k_at, own], qbd[block]) for block, _, k_at in pairs]
        dprobs = [dot_nt(v_ref[k_at, own], gbd[block]) for block, _, k_at in pairs]
        all_weights, all_dscore = [], []
        for (block, _, _), score, dprob in zip(pairs, scores, dprobs):
            log = logs[block]
            weights, dscore = [], []
            for h in range(HH):
                lanes = head(h)[0]
                w = jnp.exp2(score[:, lanes] * SCALE2 - log[h : h + 1])
                d = w * (dprob[:, lanes] - log[HH + h : HH + h + 1])
                weights.append(w.astype(jnp.bfloat16))
                dscore.append(d.astype(jnp.bfloat16))
            all_weights.append(weights)
            all_dscore.append(dscore)
        new_v = [
            dot(jnp.concatenate(weights, axis=1), gbd[block])
            for (block, _, _), weights in zip(pairs, all_weights)
        ]
        new_k = [
            dot(jnp.concatenate(dscore, axis=1), qbd[block])
            for (block, _, _), dscore in zip(pairs, all_dscore)
        ]
        new_q = [
            [dot(kt_ref[head(h)[1], k_at], dscore[h]) for h in range(HH)]
            for (_, _, k_at), dscore in zip(pairs, all_dscore)
        ]
        for (_, q_at, k_at), vs, ks, qs in zip(pairs, new_v, new_k, new_q):
            dv_acc[k_at, :] += vs
            dk_acc[k_at, :] += ks
            for h in range(HH):
                dq_acc[head(h)[1], q_at] += qs[h]

    each_pair(info, key_blocks, blocks // 2, TOGETHER, visit)
    for b in range(blocks // 2):
        at = slice(b * BLK, (b + 1) * BLK)
        grads, normed = [], []
        for r in range(2):
            block = r * (blocks // 2) + b
            lanes = slice(block * BLK, (block + 1) * BLK)
            grads.append(dq_acc[:, lanes] * SCALE)
            fade = jnp.exp2(stat[r, 0:HH, at] - logs[block, 0:HH])
            part = weighted[:, lanes].reshape(HH, HD, BLK) * fade[:, None, :]
            normed.append(part.reshape(HALF, BLK))
        for i, both in enumerate((grads, normed)):
            for k, tile in enumerate(interleave(*both)):
                tiles[i, (2 * b + k) // NX, (2 * b + k) % NX] = tile.astype(jnp.bfloat16)

    def finish(b, carry):
        at = pl.ds(pl.multiple_of(b * BLK, BLK), BLK)
        dkv[b, 0] = (dk_acc[at, :] * SCALE).astype(jnp.bfloat16)
        dkv[b, 1] = dv_acc[at, :].astype(jnp.bfloat16)
        return carry

    lax.fori_loop(0, dkv.shape[0], finish, 0, unroll=4)


def tree(n):
    steps = []
    for sign, far in ((1, n // 2), (-1, n - 1 - n // 2)):
        depth = {}
        for o in range(far, 0, -1):
            to = max(o - GROUP, 0) if o % GROUP == 0 else o - 1
            level = max(depth.get(o, 0), 2 if o - to > 1 else 0)
            depth[to] = max(depth.get(to, 0), level + 1)
            steps.append((level, sign, o, to))
    return [
        [step[1:] for step in steps if step[0] == level] for level in range(max(s[0] for s in steps) + 1)
    ]


def reduce_kernel(
    n_col, n_z, tiles, dkv, out_q, out_k, out_v, out_a, first, middle, last, mine, got, sent, come, ended, beside,
    phase_sems, swap_sems, send_sem, come_sems, end_send, end_sems, beside_sems
):
    row, me = lax.axis_index("row"), lax.axis_index("col")
    z, h, y, x = row // 2, lax.rem(row, 2), me // NX, lax.rem(me, NX)
    ny = n_col // NX
    sibling = (row + 1 - 2 * h, me)
    xs, ys = others(x, NX), others(y, ny)
    levels = tree(n_z)
    edges = [edge for level in levels for edge in level]
    ends = [edge for edge in edges if edge[2] == 0]
    inner = [edge for edge in edges if edge[2] != 0]

    def at_z(delta, core):
        return (lax.rem(z + n_z + delta, n_z) * 2 + core, me)

    def lanes_of(core):
        return pl.ds(pl.multiple_of(core * (BLK // 2), BLK // 2), BLK // 2)

    meet(
        [sibling]
        + [at_z(d, core) for d in sorted({1, n_z - 1}) for core in (h, 1 - h)]
        + [(row, y * NX + p) for p in xs]
        + [(row, p * NX + x) for p in ys]
    )

    seen = set()

    def arrived(i, slot):
        if (i, slot) not in seen:
            ref = come.at[i, slot]
            remote(ref, ref, send_sem, come_sems.at[i, slot], sibling).wait_recv()
            seen.add((i, slot))
        return come[i, slot]

    relayed = [inner.index((sign, GROUP + 1, GROUP)) for sign in (1, -1)]

    def pass_on(level):
        for edge in sorted(level, key=lambda e: -e[1]):
            for i in range(2):
                sign, o, to = edge
                if o - to > 1:
                    for slot in relayed:
                        arrived(0, slot)
                target = lax.rem(z + n_z + sign * o, n_z)
                src = dkv.at[target, i]
                from_slots = [k for k, e in enumerate(inner) if (e[0], e[2]) == (sign, o)]
                if from_slots or edge in ends:
                    value = dkv[target, i]
                    for k in from_slots:
                        value = value + arrived(i, k)
                    src = sent.at[i, edges.index(edge)]
                    src[...] = value
                if edge in inner:
                    slot = inner.index(edge)
                    remote(
                        src, come.at[i, slot], send_sem, come_sems.at[i, slot], at_z(sign * (o - to), h)
                    ).start()
                elif i == 1:
                    slot = ends.index(edge)
                    for core in range(2):
                        remote(
                            sent.at[:, edges.index(edge), core * (BLK // 2) : (core + 1) * (BLK // 2)],
                            ended.at[slot, h],
                            end_send,
                            end_sems.at[slot, h],
                            at_z(sign * o, core),
                        ).start()

    along_x = (x, NX, [(p, (row, y * NX + p)) for p in xs])
    along_y = (y, ny, [(p, (row, p * NX + x)) for p in ys])

    def phase(i, step):
        size = (along_x, along_y)[i ^ step][1]
        ref = (first, last)[step].at[i, 0 : size - 1]
        return remote(ref, ref, phase_sems.at[0, i, step], phase_sems.at[1, i, step], sibling)

    def spread(i, step):
        here, size, peers = (along_x, along_y)[i ^ step]
        for p, device in peers:
            src = middle.at[i, p] if step else (tiles.at[0, :, p] if i == 0 else tiles.at[1, p])
            dst = (first, last)[step].at[i, here]
            remote(src, dst, phase_sems.at[0, i, step], phase_sems.at[1, i, step], device).start()
        if step:
            last[i, here] = middle[i, here]
        else:
            first[i, here] = tiles[0, :, x] if i == 0 else tiles[1, y]

    def summed(i, step, at):
        size = (along_x, along_y)[i ^ step][1]
        refs = [first[i, k, at] if step == 0 else last[i, k] for k in range(size)]
        return functools.reduce(jnp.add, [ref.astype(jnp.float32) for ref in refs])

    pass_on(levels[0])
    aside = remote(dkv.at[z, :, lanes_of(1 - h)], beside, beside_sems.at[0], beside_sems.at[1], sibling)
    aside.start()
    for i in range(2):
        spread(i, 0)
    finishes = []
    for s in range(1, max(len(levels), 4)):
        if s < len(levels):
            pass_on(levels[s])
        for i in range(2):
            if s == 2:
                phase(i, 0).wait_recv()
                for b in range((along_y, along_x)[i][1]):
                    middle[i, b] = summed(i, 0, b).astype(jnp.bfloat16)
                spread(i, 1)
            if s == 3:
                phase(i, 1).wait_recv()
                out = (out_q, out_a)[i]
                finishes.append(
                    swap_rows(summed(i, 1, 0).T, out, mine.at[i], got.at[i], swap_sems.at[i], h, sibling)
                )
    aside.wait_recv()
    for finish in finishes:
        finish()
    totals = [dkv[z, :, lanes_of(h)].astype(jnp.float32), beside[...].astype(jnp.float32)]
    for c in range(len(ends)):
        for k, core in enumerate((h, 1 - h)):
            ref = ended.at[c, core]
            remote(ref, ref, end_send, end_sems.at[c, core], sibling).wait_recv()
            totals[k] = totals[k] + ended[c, core].astype(jnp.float32)
    for total, core in zip(totals, (h, 1 - h)):
        out_k[:, half_at(core)] = total[0].astype(jnp.bfloat16)
        out_v[:, half_at(core)] = total[1].astype(jnp.bfloat16)
    aside.wait_send()
    remote(come, come, send_sem, come_sems.at[0, 0], sibling).wait_send()
    remote(ended, ended, end_send, end_sems.at[0, 0], sibling).wait_send()
    for i in range(2):
        for step in range(2):
            phase(i, step).wait_send()


def leave_kernel(*refs):
    half = len(refs) // 2
    for src, dst in zip(refs[:half], refs[half:]):
        dst[0] = src[...]


def fwd_scratch(blocks, lanes):
    f32 = jnp.float32
    rows = blocks * BLK
    return [
        pltpu.VMEM((HALF, lanes), jnp.bfloat16),
        pltpu.VMEM((HH, rows + BLK), f32),
        pltpu.VMEM((HH, rows + BLK), f32),
    ]


def bwd_scratch(blocks, lanes):
    f32 = jnp.float32
    rows = blocks * BLK
    return [
        pltpu.VMEM((blocks + 1, H, BLK), f32),
        pltpu.VMEM((HALF, rows + BLK), f32),
        pltpu.VMEM((lanes, HALF), f32),
        pltpu.VMEM((lanes, HALF), f32),
    ]


def shards(n_row, n_col, queries, key_lanes, values, grad_out, pattern, counts):
    bf16, f32 = jnp.bfloat16, jnp.float32
    dma = pltpu.SemaphoreType.DMA
    shape = jax.ShapeDtypeStruct
    own_q, own_g, keys, vals = queries[0], grad_out[0], key_lanes[0], values[0]
    own_rows, lanes = own_q.shape[0], keys.shape[0]
    rows = own_rows * n_col * 2
    blocks, key_blocks, n_z, ny = rows // BLK, lanes // BLK, n_row // 2, n_col // NX

    own_cells = jnp.pad(pattern[0].astype(bf16), ((0, 0), (0, D - pattern.shape[2])))
    own_count = jnp.pad(counts.astype(bf16), ((0, 14), (0, D - 1)))
    own = jnp.concatenate([own_q, own_g, own_cells, own_count], axis=0)
    all_q, all_g, info = call(
        functools.partial(gather_kernel, n_col),
        "gather_lanes",
        (shape((2, ny, NX, own_rows, HALF), bf16),) * 2 + (shape((2, 16, BLK), jnp.int32),),
        [vmem],
        [pltpu.VMEM((2, 16, HALF), bf16), dma((2, 3)), dma((2, 4))],
        0,
    )(own)
    all_q, all_g = all_q.reshape(rows, HALF), all_g.reshape(rows, HALF)

    folded = (H, rows // 2 * 3 // 2)
    by_head = shape((blocks + 1, HH * BLK, HALF), bf16)
    weighted, stat, qbd = call(
        functools.partial(forward_kernel, key_blocks),
        "forward_pairs",
        (shape((HALF, rows + BLK), f32), shape((2, *folded), f32), by_head),
        [smem] + [vmem] * 4,
        fwd_scratch(blocks, lanes),
    )(info, all_q, all_g, keys, vals)

    logs, gbd, keys_t = call(
        functools.partial(combine_kernel, n_col),
        "combine_rows",
        (shape((blocks, H, BLK), f32), by_head, shape((HALF, lanes), bf16)),
        [vmem] * 3,
        [
            pltpu.VMEM((2, 2, max(NX, ny), *folded), f32),
            pltpu.VMEM((2, *folded), f32),
            dma((2, 2, 2)),
        ],
        1,
    )(stat, all_g, keys)

    tiles, dkv = call(
        functools.partial(backward_kernel, key_blocks),
        "backward_pairs",
        (shape((2, ny, NX, HALF, BLK), bf16), shape((key_blocks, 2, BLK, HALF), bf16)),
        [smem] + [vmem] * 8,
        bwd_scratch(blocks, lanes),
    )(info, qbd, gbd, keys, vals, keys_t, logs, weighted, stat)

    side = max(NX, ny)
    edges = [edge for level in tree(n_z) for edge in level]
    n_sent, n_ends = len(edges), sum(edge[2] == 0 for edge in edges)
    grads = call(
        functools.partial(reduce_kernel, n_col, n_z),
        "reduce_gradients",
        (shape((own_rows, D), bf16),) * 4,
        [vmem] * 2,
        [
            pltpu.VMEM((2, side, side, HALF, BLK), bf16),
            pltpu.VMEM((2, side, HALF, BLK), bf16),
            pltpu.VMEM((2, side, HALF, BLK), bf16),
            pltpu.VMEM((2, BLK, HALF), bf16),
            pltpu.VMEM((2, own_rows, HALF), bf16),
            pltpu.VMEM((2, n_sent, BLK, HALF), bf16),
            pltpu.VMEM((2, n_sent - n_ends, BLK, HALF), bf16),
            pltpu.VMEM((n_ends, 2, 2, own_rows, HALF), bf16),
            pltpu.VMEM((2, own_rows, HALF), bf16),
            dma((2, 2, 2)),
            dma((2, 2)),
            dma,
            dma((2, n_sent - n_ends)),
            dma,
            dma((n_ends, 2)),
            dma((2,)),
        ],
        2,
    )(tiles, dkv)
    grad_q, grad_k, grad_v, attended = call(
        leave_kernel, "leave", (shape((1, own_rows, D), bf16),) * 4, [vmem] * 4, []
    )(*grads)
    return attended, grad_q, grad_k, grad_v


def solution(mesh):
    return jax.shard_map(
        functools.partial(shards, mesh.shape["row"], mesh.shape["col"]),
        mesh=mesh,
        in_specs=(
            P("row", "col", None),
            P("col", None, None),
            P("col", None, None),
            P("row", "col", None),
            P("row", "col", None),
            P("row", "col"),
        ),
        out_specs=(
            P("row", "col", None),
            P("row", "col", None),
            P("col", "row", None),
            P("col", "row", None),
        ),
        check_vma=False,
    )
```

```python
import functools
import math

import jax
import jax.numpy as jnp
from jax import lax
from jax.experimental import pallas as pl
from jax.experimental.pallas import tpu as pltpu
from jax.sharding import PartitionSpec as P

D = 256
H = 8
HD = 32
BLK = 128
HALF = D // 2
HH = H // 2
NX = 4
TOGETHER = 8
GROUP = 3
MESH = pl.DeviceIdType.MESH
SCALE = 1.0 / math.sqrt(HD)
LOG2E = math.log2(math.e)
SCALE2 = SCALE * LOG2E
NEG = -1e30
VMEM_LIMIT = 32 * 1024 * 1024

vmem = pl.BlockSpec(memory_space=pltpu.VMEM)
smem = pl.BlockSpec(memory_space=pltpu.SMEM)


def call(kernel, name, out_shape, in_specs, scratch, collective_id=None, micros=10):
    return pl.pallas_call(
        kernel,
        name=name,
        out_shape=out_shape,
        in_specs=in_specs,
        out_specs=jax.tree.map(lambda _: vmem, out_shape),
        scratch_shapes=scratch,
        cost_estimate=pl.CostEstimate(
            flops=micros * 10**9, bytes_accessed=micros * 10**6, transcendentals=0
        ),
        compiler_params=pltpu.CompilerParams(
            collective_id=collective_id,
            has_side_effects=collective_id is not None,
            vmem_limit_bytes=VMEM_LIMIT,
        ),
    )


def meet(peers):
    barrier = pltpu.get_barrier_semaphore()
    for peer in peers:
        pl.semaphore_signal(barrier, inc=1, device_id=peer, device_id_type=MESH)
    pl.semaphore_wait(barrier, len(peers))


def remote(src, dst, send_sem, recv_sem, device):
    return pltpu.make_async_remote_copy(
        src_ref=src,
        dst_ref=dst,
        send_sem=send_sem,
        recv_sem=recv_sem,
        device_id=device,
        device_id_type=MESH,
    )


def others(me, n):
    return [lax.rem(me + k, n) for k in range(1, n)]


def farthest(me, n):
    return [lax.rem(me + k, n) for k in sorted(range(1, n), key=lambda k: -min(k, n - k))]


def block_diagonal(pairs):
    blocks = pairs[0][1].shape[0] - 1
    lane = lax.broadcasted_iota(jnp.int32, (BLK, HALF), 1)
    masks = [
        jnp.where((lane >= h * HD) & (lane < (h + 1) * HD), 1.0, 0.0).astype(jnp.bfloat16)
        for h in range(HH)
    ]

    def one(b, carry):
        rows = pl.ds(pl.multiple_of(b * BLK, BLK), BLK)
        for ref, out in pairs:
            block = ref[rows, :]
            for h in range(HH):
                out[b, h * BLK : (h + 1) * BLK, :] = block * masks[h]
        return carry

    lax.fori_loop(0, blocks, one, 0, unroll=4)
    for _, out in pairs:
        out[blocks] = jnp.zeros(out.shape[1:], out.dtype)


def interleave(a, b):
    low = lax.broadcasted_iota(jnp.int32, a.shape, 1) < BLK // 2
    turned_a, turned_b = pltpu.roll(a, BLK // 2, 1), pltpu.roll(b, BLK // 2, 1)
    return jnp.where(low, a, turned_b), jnp.where(low, turned_a, b)


def dot_nt(a, b):
    return lax.dot_general(a, b, (((1,), (1,)), ((), ())), preferred_element_type=jnp.float32)


def dot(a, b):
    return jnp.dot(a, b, preferred_element_type=jnp.float32)


def half_at(h):
    return pl.ds(pl.multiple_of(h * HALF, HALF), HALF)


def turn_blocks(src, half, out):
    def one(b, carry):
        rows = pl.ds(pl.multiple_of(b * BLK, BLK), BLK)
        out[:, rows] = src[rows, half].T
        return carry

    lax.fori_loop(0, src.shape[0] // BLK, one, 0, unroll=4)


def gather_kernel(n_col, own_ref, qo, go, info, tables, swap_sems, sems):
    row, me = lax.axis_index("row"), lax.axis_index("col")
    h, y, x = lax.rem(row, 2), me // NX, lax.rem(me, NX)
    ny = n_col // NX
    rows = qo.shape[3]
    sibling = (row + 1 - 2 * h, me)
    along_x = [(row, y * NX + p) for p in farthest(x, NX)]
    along_y = [(row, p * NX + x) for p in farthest(y, ny)]
    meet([sibling] + along_x + along_y)
    swaps = [
        remote(src, dst, swap_sems.at[0, i], swap_sems.at[1, i], sibling)
        for i, (src, dst) in enumerate(
            (
                (own_ref.at[0:rows, half_at(1 - h)], qo.at[h, y, x]),
                (own_ref.at[rows : 2 * rows, half_at(1 - h)], go.at[h, y, x]),
                (own_ref.at[2 * rows :, 0:HALF], tables.at[h]),
            )
        )
    ]
    for copy in swaps:
        copy.start()
    qo[h, y, x] = own_ref[0:rows, half_at(h)]
    go[h, y, x] = own_ref[rows : 2 * rows, half_at(h)]
    tables[h] = own_ref[2 * rows :, 0:HALF]

    def send(i, ref, peers):
        for p in peers:
            remote(ref, ref, sems.at[0, i], sems.at[1, i], p).start()

    def all_of(i, ref):
        return remote(ref, ref, sems.at[0, i], sems.at[1, i], sibling)

    phases = [qo.at[:, y, 0 : NX - 1], go.at[:, 0 : ny - 1, x], qo.at[:, 0 : ny - 1], go.at[:, :, 0 : NX - 1]]
    swaps[0].wait_recv()
    send(0, qo.at[:, y, x], along_x)
    swaps[1].wait_recv()
    send(1, go.at[:, y, x], along_y)
    swaps[2].wait_recv()
    table = tables[...].astype(jnp.float32).astype(jnp.int32)
    mark = lax.broadcasted_iota(jnp.int32, table.shape, 1) == 2
    info[...] = jnp.where(mark, h, table)
    all_of(0, phases[0]).wait_recv()
    send(2, qo.at[:, y], along_y)
    all_of(1, phases[1]).wait_recv()
    send(3, go.at[:, :, x], along_x)
    all_of(2, phases[2]).wait_recv()
    all_of(3, phases[3]).wait_recv()
    for i, ref in enumerate(phases):
        all_of(i, ref).wait_send()
    for copy in swaps:
        copy.wait_send()


def each_pair(info, key_blocks, q_blocks, together, visit):
    n_first = info[0, 1, 0]
    n_pairs = n_first + info[1, 1, 0]

    def group(i, carry):
        found = []
        for u in range(together):
            j = i * together + u
            second = (j >= n_first).astype(jnp.int32)
            real = j < n_pairs
            cell = info[second, 0, jnp.where(real, j - second * n_first, 0)]
            block = jnp.where(real, cell // key_blocks + second * q_blocks, 2 * q_blocks)
            q_at = pl.ds(pl.multiple_of(block * BLK, BLK), BLK)
            k_at = pl.ds(pl.multiple_of(cell % key_blocks * BLK, BLK), BLK)
            found.append((block, q_at, k_at))
        visit(found)
        return carry

    lax.fori_loop(0, (n_pairs + together - 1) // together, group, 0)


def head(h):
    return slice(h * BLK, (h + 1) * BLK), slice(h * HD, (h + 1) * HD)


def forward_kernel(key_blocks, info, q_ref, g_ref, k_ref, v_ref, acc, stat, qbd, vt_ref, top, tot):
    own = half_at(info[0, 2, 0])
    turn_blocks(v_ref, own, vt_ref)
    blocks = qbd.shape[0] - 1
    block_diagonal(((q_ref, qbd),))
    acc[...] = jnp.zeros_like(acc)
    tot[...] = jnp.zeros_like(tot)
    top[...] = jnp.full_like(top, NEG)

    def visit(pairs):
        scores = [dot_nt(k_ref[k_at, own], qbd[block]) for block, _, k_at in pairs]
        probs, fades, sums = [], [], []
        for (_, q_at, _), score in zip(pairs, scores):
            best = [jnp.max(score[:, head(h)[0]], axis=0, keepdims=True) for h in range(HH)]
            old = top[:, q_at]
            new = jnp.maximum(old, jnp.concatenate(best, axis=0) * SCALE2)
            top[:, q_at] = new
            fades.append(jnp.exp2(old - new))
            prob = [jnp.exp2(score[:, head(h)[0]] * SCALE2 - new[h : h + 1]) for h in range(HH)]
            sums.append([jnp.sum(p, axis=0, keepdims=True) for p in prob])
            probs.append([p.astype(jnp.bfloat16) for p in prob])
        mixed = [
            [dot(vt_ref[head(h)[1], k_at], prob[h]) for h in range(HH)]
            for (_, _, k_at), prob in zip(pairs, probs)
        ]
        for (_, q_at, _), fade, total, mix in zip(pairs, fades, sums, mixed):
            tot[:, q_at] = tot[:, q_at] * fade + jnp.concatenate(total, axis=0)
            for h in range(HH):
                at = head(h)[1]
                acc[at, q_at] = acc[at, q_at] * fade[h : h + 1] + mix[h]

    each_pair(info, key_blocks, blocks // 2, TOGETHER, visit)
    lanes = blocks // 2 * BLK
    for b in range(blocks):
        r, at = divmod(b, blocks // 2)
        from_lane, to_lane = b * BLK, at * BLK
        grad = g_ref[from_lane : from_lane + BLK, :].astype(jnp.float32).T
        dots = jnp.sum((grad * acc[:, from_lane : from_lane + BLK]).reshape(HH, HD, BLK), axis=1)
        stat[r, 0:HH, to_lane : to_lane + BLK] = top[:, from_lane : from_lane + BLK]
        stat[r, HH:H, to_lane : to_lane + BLK] = tot[:, from_lane : from_lane + BLK]
        fold, to_lane = divmod(to_lane, lanes // 2)
        stat[r, fold * HH : (fold + 1) * HH, lanes + to_lane : lanes + to_lane + BLK] = dots


def swap_rows(tile, out, mine, got, sems, h, sibling):
    rows = BLK // 2
    mine[...] = tile.astype(mine.dtype)
    copy = remote(
        mine.at[pl.ds(pl.multiple_of((1 - h) * rows, rows), rows)], got, sems.at[0], sems.at[1], sibling
    )
    copy.start()

    def finish():
        out[:, half_at(h)] = mine[pl.ds(pl.multiple_of(h * rows, rows), rows), :]
        copy.wait_recv()
        out[:, half_at(1 - h)] = got[...]
        copy.wait_send()

    return finish


def combine_kernel(n, stat, g_ref, k_ref, logs, gbd, kt_ref, got, middle, sems):
    row, me = lax.axis_index("row"), lax.axis_index("col")
    y, x = me // NX, lax.rem(me, NX)
    ny = n // NX
    lanes = stat.shape[2] * 2 // 3
    along_x = (x, NX, [(row, y * NX + p) for p in farthest(x, NX)])
    along_y = (y, ny, [(row, p * NX + x) for p in farthest(y, ny)])
    meet(along_x[2] + along_y[2])

    def start(phase, r, src):
        here, _, peers = (along_x, along_y)[phase ^ r]
        for p in peers:
            dst = got.at[phase, r, here]
            remote(src, dst, sems.at[0, phase, r], sems.at[1, phase, r], p).start()
        got[phase, r, here] = src[...]

    def all_of(phase, r):
        _, size, peers = (along_x, along_y)[phase ^ r]
        ref = got.at[phase, r, 0 : size - 1]
        return remote(ref, ref, sems.at[0, phase, r], sems.at[1, phase, r], peers[0])

    def merged(phase, r):
        size = (along_x, along_y)[phase ^ r][1]
        parts = [got[phase, r, i] for i in range(size)]
        top = functools.reduce(jnp.maximum, [part[0:HH, :lanes] for part in parts])
        tot, dots = 0.0, 0.0
        for part in parts:
            fade = jnp.exp2(part[0:HH, :lanes] - top)
            tot = tot + part[HH:H, :lanes] * fade
            fold = jnp.concatenate([fade[:, : lanes // 2], fade[:, lanes // 2 :]], axis=0)
            dots = dots + part[:, lanes:] * fold
        return top, tot, dots

    for r in range(2):
        start(0, r, stat.at[r])
    block_diagonal(((g_ref, gbd),))
    for r in range(2):
        all_of(0, r).wait_recv()
        top, tot, dots = merged(0, r)
        middle[r, 0:HH, :lanes] = top
        middle[r, HH:H, :lanes] = tot
        middle[r, :, lanes:] = dots
        start(1, r, middle.at[r])
    turn_blocks(k_ref, half_at(lax.rem(row, 2)), kt_ref)
    for r in range(2):
        all_of(1, r).wait_recv()
        top, tot, dots = merged(1, r)
        total = top + jnp.log(tot) * LOG2E
        dots = jnp.concatenate([dots[0:HH], dots[HH:H]], axis=1) / tot
        for b in range(lanes // BLK):
            at = slice(b * BLK, (b + 1) * BLK)
            logs[r * (lanes // BLK) + b, 0:HH] = total[:, at]
            logs[r * (lanes // BLK) + b, HH:H] = dots[:, at]
    for phase in range(2):
        for r in range(2):
            all_of(phase, r).wait_send()


def backward_kernel(
    key_blocks, info, qbd, gbd, k_ref, v_ref, kt_ref, logs_ref, dq_acc, dkv, logs, dk_acc, dv_acc
):
    blocks = qbd.shape[0] - 1
    own = half_at(info[0, 2, 0])
    dq_acc[...] = jnp.zeros_like(dq_acc)
    dk_acc[...] = jnp.zeros_like(dk_acc)
    dv_acc[...] = jnp.zeros_like(dv_acc)
    logs[0:blocks] = logs_ref[...]
    logs[blocks] = jnp.zeros(logs.shape[1:], logs.dtype)

    def visit(pairs):
        scores = [dot_nt(k_ref[k_at, own], qbd[block]) for block, _, k_at in pairs]
        dprobs = [dot_nt(v_ref[k_at, own], gbd[block]) for block, _, k_at in pairs]
        all_weights, all_dscore = [], []
        for (block, _, _), score, dprob in zip(pairs, scores, dprobs):
            log = logs[block]
            weights, dscore = [], []
            for h in range(HH):
                lanes = head(h)[0]
                w = jnp.exp2(score[:, lanes] * SCALE2 - log[h : h + 1])
                d = w * (dprob[:, lanes] - log[HH + h : HH + h + 1])
                weights.append(w.astype(jnp.bfloat16))
                dscore.append(d.astype(jnp.bfloat16))
            all_weights.append(weights)
            all_dscore.append(dscore)
        new_v = [
            dot(jnp.concatenate(weights, axis=1), gbd[block])
            for (block, _, _), weights in zip(pairs, all_weights)
        ]
        new_k = [
            dot(jnp.concatenate(dscore, axis=1), qbd[block])
            for (block, _, _), dscore in zip(pairs, all_dscore)
        ]
        new_q = [
            [dot(kt_ref[head(h)[1], k_at], dscore[h]) for h in range(HH)]
            for (_, _, k_at), dscore in zip(pairs, all_dscore)
        ]
        for (_, q_at, k_at), vs, ks, qs in zip(pairs, new_v, new_k, new_q):
            dv_acc[k_at, :] += vs
            dk_acc[k_at, :] += ks
            for h in range(HH):
                dq_acc[head(h)[1], q_at] += qs[h]

    each_pair(info, key_blocks, blocks // 2, TOGETHER, visit)
    def finish(b, carry):
        at = pl.ds(pl.multiple_of(b * BLK, BLK), BLK)
        dkv[b, 0] = (dk_acc[at, :] * SCALE).astype(jnp.bfloat16)
        dkv[b, 1] = dv_acc[at, :].astype(jnp.bfloat16)
        return carry

    lax.fori_loop(0, dkv.shape[0], finish, 0, unroll=4)


def make_tiles(dq_acc, weighted, stat, logs, tiles):
    blocks = logs.shape[0]
    for b in range(blocks // 2):
        at = slice(b * BLK, (b + 1) * BLK)
        grads, normed = [], []
        for r in range(2):
            block = r * (blocks // 2) + b
            lanes = slice(block * BLK, (block + 1) * BLK)
            grads.append(dq_acc[:, lanes] * SCALE)
            fade = jnp.exp2(stat[r, 0:HH, at] - logs[block, 0:HH])
            part = weighted[:, lanes].reshape(HH, HD, BLK) * fade[:, None, :]
            normed.append(part.reshape(HALF, BLK))
        for i, both in enumerate((grads, normed)):
            for k, tile in enumerate(interleave(*both)):
                tiles[i, (2 * b + k) // NX, (2 * b + k) % NX] = tile.astype(jnp.bfloat16)


def tree(n):
    steps = []
    for sign, far in ((1, n // 2), (-1, n - 1 - n // 2)):
        depth = {}
        for o in range(far, 0, -1):
            to = max(o - GROUP, 0) if o % GROUP == 0 else o - 1
            level = max(depth.get(o, 0), 2 if o - to > 1 else 0)
            depth[to] = max(depth.get(to, 0), level + 1)
            steps.append((level, sign, o, to))
    last = max(step[0] for step in steps)
    return [
        [step[1:] for step in steps if level == (step[0] if step[3] else last)] for level in range(last + 1)
    ]


def reduce_kernel(
    n_col, n_z, dq_acc, dkv, weighted, stat, logs, out_q, out_k, out_v, out_a, tiles, first, middle, last, mine, got, sent, come, ended, beside,
    phase_sems, swap_sems, send_sem, come_sems, end_send, end_sems, beside_sems
):
    row, me = lax.axis_index("row"), lax.axis_index("col")
    z, h, y, x = row // 2, lax.rem(row, 2), me // NX, lax.rem(me, NX)
    ny = n_col // NX
    sibling = (row + 1 - 2 * h, me)
    xs, ys = others(x, NX), others(y, ny)
    levels = tree(n_z)
    edges = [edge for level in levels for edge in level]
    ends = [edge for edge in edges if edge[2] == 0]
    inner = [edge for edge in edges if edge[2] != 0]

    def at_z(delta, core):
        return (lax.rem(z + n_z + delta, n_z) * 2 + core, me)

    def lanes_of(core):
        return pl.ds(pl.multiple_of(core * (BLK // 2), BLK // 2), BLK // 2)

    along_x = (x, NX, [(row, y * NX + p) for p in xs])
    along_y = (y, ny, [(row, p * NX + x) for p in ys])
    near = [line[2][k] for line in (along_x, along_y) for k in (0, -1)]
    meet([sibling, at_z(1, h), at_z(-1, h)] + near)

    seen = set()

    def arrived(i, slot):
        if (i, slot) not in seen:
            ref = come.at[i, slot]
            remote(ref, ref, send_sem, come_sems.at[i, slot], sibling).wait_recv()
            seen.add((i, slot))
        return come[i, slot]

    relayed = [inner.index((sign, GROUP + 1, GROUP)) for sign in (1, -1)]

    def pass_on(level):
        for edge in sorted(level, key=lambda e: -e[1]):
            for i in range(2):
                sign, o, to = edge
                if o - to > 1:
                    for slot in relayed:
                        arrived(0, slot)
                target = lax.rem(z + n_z + sign * o, n_z)
                src = dkv.at[target, i]
                from_slots = [k for k, e in enumerate(inner) if (e[0], e[2]) == (sign, o)]
                if from_slots or edge in ends:
                    value = dkv[target, i]
                    for k in from_slots:
                        value = value + arrived(i, k)
                    src = sent.at[i, edges.index(edge)]
                    src[...] = value
                if edge in inner:
                    slot = inner.index(edge)
                    remote(
                        src, come.at[i, slot], send_sem, come_sems.at[i, slot], at_z(sign * (o - to), h)
                    ).start()
                elif i == 1:
                    slot = ends.index(edge)
                    for core in range(2):
                        remote(
                            sent.at[:, edges.index(edge), core * (BLK // 2) : (core + 1) * (BLK // 2)],
                            ended.at[slot, h],
                            end_send,
                            end_sems.at[slot, h],
                            at_z(sign * o, core),
                        ).start()

    def phase(i, step, part):
        size = (along_x, along_y)[i ^ step][1] - 1
        count = size if step else (2, size - 2)[part]
        ref = (first, last)[step].at[i, 0:count]
        return remote(ref, ref, phase_sems.at[0, i, step, part], phase_sems.at[1, i, step, part], sibling)

    def spread(i, step, part):
        here, _, peers = (along_x, along_y)[i ^ step]
        chosen = peers if step else (peers[:1] + peers[-1:], peers[1:-1])[part]
        for device in chosen:
            p = device[1] // NX if (i ^ step) else lax.rem(device[1], NX)
            src = middle.at[i, p] if step else (tiles.at[0, :, p] if i == 0 else tiles.at[1, p])
            dst = (first, last)[step].at[i, here]
            remote(
                src, dst, phase_sems.at[0, i, step, part], phase_sems.at[1, i, step, part], device
            ).start()
        if step:
            last[i, here] = middle[i, here]
        elif part == 0:
            first[i, here] = tiles[0, :, x] if i == 0 else tiles[1, y]

    def summed(i, step, at):
        size = (along_x, along_y)[i ^ step][1]
        refs = [first[i, k, at] if step == 0 else last[i, k] for k in range(size)]
        return functools.reduce(jnp.add, [ref.astype(jnp.float32) for ref in refs])

    aside = remote(dkv.at[z, :, lanes_of(1 - h)], beside, beside_sems.at[0], beside_sems.at[1], sibling)
    finishes = []
    for s, level in enumerate(levels):
        if s == len(levels) - 1:
            aside.start()
            aside.wait_recv()
        pass_on(level)
        if s == 0:
            make_tiles(dq_acc, weighted, stat, logs, tiles)
        for i in range(2):
            if s == 0:
                spread(i, 0, 0)
            if s == 1:
                phase(i, 0, 0).wait_recv()
                spread(i, 0, 1)
        for i in range(2):
            if s == 2:
                phase(i, 0, 1).wait_recv()
                for b in range((along_y, along_x)[i][1]):
                    middle[i, b] = summed(i, 0, b).astype(jnp.bfloat16)
                spread(i, 1, 0)
    for i, out in enumerate((out_q, out_a)):
        phase(i, 1, 0).wait_recv()
        finishes.append(swap_rows(summed(i, 1, 0).T, out, mine.at[i], got.at[i], swap_sems.at[i], h, sibling))
    for finish in finishes:
        finish()
    totals = [dkv[z, :, lanes_of(h)].astype(jnp.float32), beside[...].astype(jnp.float32)]
    for c in range(len(ends)):
        for k, core in enumerate((h, 1 - h)):
            ref = ended.at[c, core]
            remote(ref, ref, end_send, end_sems.at[c, core], sibling).wait_recv()
            totals[k] = totals[k] + ended[c, core].astype(jnp.float32)
    for total, core in zip(totals, (h, 1 - h)):
        out_k[:, half_at(core)] = total[0].astype(jnp.bfloat16)
        out_v[:, half_at(core)] = total[1].astype(jnp.bfloat16)
    aside.wait_send()
    remote(come, come, send_sem, come_sems.at[0, 0], sibling).wait_send()
    remote(ended, ended, end_send, end_sems.at[0, 0], sibling).wait_send()
    for i in range(2):
        phase(i, 0, 0).wait_send()
        phase(i, 0, 1).wait_send()
        phase(i, 1, 0).wait_send()


def leave_kernel(*refs):
    half = len(refs) // 2
    for src, dst in zip(refs[:half], refs[half:]):
        dst[0] = src[...]


def fwd_scratch(blocks, lanes):
    f32 = jnp.float32
    rows = blocks * BLK
    return [
        pltpu.VMEM((HALF, lanes), jnp.bfloat16),
        pltpu.VMEM((HH, rows + BLK), f32),
        pltpu.VMEM((HH, rows + BLK), f32),
    ]


def bwd_scratch(blocks, lanes):
    f32 = jnp.float32
    return [
        pltpu.VMEM((blocks + 1, H, BLK), f32),
        pltpu.VMEM((lanes, HALF), f32),
        pltpu.VMEM((lanes, HALF), f32),
    ]


def shards(n_row, n_col, queries, key_lanes, values, grad_out, pattern, counts):
    bf16, f32 = jnp.bfloat16, jnp.float32
    dma = pltpu.SemaphoreType.DMA
    shape = jax.ShapeDtypeStruct
    own_q, own_g, keys, vals = queries[0], grad_out[0], key_lanes[0], values[0]
    own_rows, lanes = own_q.shape[0], keys.shape[0]
    rows = own_rows * n_col * 2
    blocks, key_blocks, n_z, ny = rows // BLK, lanes // BLK, n_row // 2, n_col // NX

    own_cells = jnp.pad(pattern[0].astype(bf16), ((0, 0), (0, D - pattern.shape[2])))
    own_count = jnp.pad(counts.astype(bf16), ((0, 14), (0, D - 1)))
    own = jnp.concatenate([own_q, own_g, own_cells, own_count], axis=0)
    all_q, all_g, info = call(
        functools.partial(gather_kernel, n_col),
        "gather_lanes",
        (shape((2, ny, NX, own_rows, HALF), bf16),) * 2 + (shape((2, 16, BLK), jnp.int32),),
        [vmem],
        [pltpu.VMEM((2, 16, HALF), bf16), dma((2, 3)), dma((2, 4))],
        0,
    )(own)
    all_q, all_g = all_q.reshape(rows, HALF), all_g.reshape(rows, HALF)

    folded = (H, rows // 2 * 3 // 2)
    by_head = shape((blocks + 1, HH * BLK, HALF), bf16)
    weighted, stat, qbd = call(
        functools.partial(forward_kernel, key_blocks),
        "forward_pairs",
        (shape((HALF, rows + BLK), f32), shape((2, *folded), f32), by_head),
        [smem] + [vmem] * 4,
        fwd_scratch(blocks, lanes),
    )(info, all_q, all_g, keys, vals)

    logs, gbd, keys_t = call(
        functools.partial(combine_kernel, n_col),
        "combine_rows",
        (shape((blocks, H, BLK), f32), by_head, shape((HALF, lanes), bf16)),
        [vmem] * 3,
        [
            pltpu.VMEM((2, 2, max(NX, ny), *folded), f32),
            pltpu.VMEM((2, *folded), f32),
            dma((2, 2, 2)),
        ],
        1,
    )(stat, all_g, keys)

    dq, dkv = call(
        functools.partial(backward_kernel, key_blocks),
        "backward_pairs",
        (shape((HALF, rows + BLK), f32), shape((key_blocks, 2, BLK, HALF), bf16)),
        [smem] + [vmem] * 6,
        bwd_scratch(blocks, lanes),
    )(info, qbd, gbd, keys, vals, keys_t, logs)

    side = max(NX, ny)
    edges = [edge for level in tree(n_z) for edge in level]
    n_sent, n_ends = len(edges), sum(edge[2] == 0 for edge in edges)
    grads = call(
        functools.partial(reduce_kernel, n_col, n_z),
        "reduce_gradients",
        (shape((own_rows, D), bf16),) * 4,
        [vmem] * 5,
        [
            pltpu.VMEM((2, ny, NX, HALF, BLK), bf16),
            pltpu.VMEM((2, side, side, HALF, BLK), bf16),
            pltpu.VMEM((2, side, HALF, BLK), bf16),
            pltpu.VMEM((2, side, HALF, BLK), bf16),
            pltpu.VMEM((2, BLK, HALF), bf16),
            pltpu.VMEM((2, own_rows, HALF), bf16),
            pltpu.VMEM((2, n_sent, BLK, HALF), bf16),
            pltpu.VMEM((2, n_sent - n_ends, BLK, HALF), bf16),
            pltpu.VMEM((n_ends, 2, 2, own_rows, HALF), bf16),
            pltpu.VMEM((2, own_rows, HALF), bf16),
            dma((2, 2, 2, 2)),
            dma((2, 2)),
            dma,
            dma((2, n_sent - n_ends)),
            dma,
            dma((n_ends, 2)),
            dma((2,)),
        ],
        2,
    )(dq, dkv, weighted, stat, logs)
    grad_q, grad_k, grad_v, attended = call(
        leave_kernel, "leave", (shape((1, own_rows, D), bf16),) * 4, [vmem] * 4, []
    )(*grads)
    return attended, grad_q, grad_k, grad_v


def solution(mesh):
    return jax.shard_map(
        functools.partial(shards, mesh.shape["row"], mesh.shape["col"]),
        mesh=mesh,
        in_specs=(
            P("row", "col", None),
            P("col", None, None),
            P("col", None, None),
            P("row", "col", None),
            P("row", "col", None),
            P("row", "col"),
        ),
        out_specs=(
            P("row", "col", None),
            P("row", "col", None),
            P("col", "row", None),
            P("col", "row", None),
        ),
        check_vma=False,
    )
```
